128 devices in a mesh: row: 16 (over y, z_lo, core), col: 8 (over x, z_hi).
Axes of the slice: x: 4, y: 4, z: 4 (z_hi: 2, z_lo: 2; z = z_hi * 2 + z_lo), core: 2. Of those that a mesh axis runs over, the one named last changes fastest.
Arguments:
- tokens: bfloat16 [512, 16384], P('col', 'row'), may hold values from -6 to 6
- weight: bfloat16 [16384, 26624], P('row', 'col'), may hold values from -0.046875 to 0.046875
- adapter_down_matrix: bfloat16 [16384, 64], P('row'), may hold values from -0.046875 to 0.046875
- adapter_up_matrix: bfloat16 [64, 26624], P(None, 'col'), may hold values from -0.75 to 0.75
- grad_out: bfloat16 [512, 26624], P('row', 'col'), may hold values from -6 to 6
- tile_list: int32 [16, 8, 156], P('row', 'col'), may hold values from 0 to 208, as said below
Outputs:
- projected: bfloat16 [512, 26624], P('row', 'col')
- grad_tokens: bfloat16 [512, 16384], P('col', 'row')
- grad_weight: bfloat16 [16384, 26624], P('row', 'col')
The draws below stay inside these ranges and needn't reach their ends.
Inputs may be any that keep to these rules, and one draw needn't show every extreme that they name: Each list tile_list[r, c] holds the distinct kept tile numbers of block (r, c) in increasing order, followed by the filler 208; a block keeps between 52 and 156 tiles.
All inputs are finite; a program needn't handle non-finite values.
Results may differ from the reference program's by a relative error of at most 0.001.
Values may be sent and summed in bfloat16 or wider, within the bound.
A program may use at most 128 MiB of HBM per device.

```python
import jax
import jax.numpy as jnp
from jax import lax

MODEL_WIDTH = 16384
HIDDEN_WIDTH = 26624
ADAPTER_RANK = 64
TILE_SIDE = 128
TOKENS = 512
GRID_ROW = 16
GRID_COL = 8
TILES_DEV = 208
TILE_CAP = 156


def draw_tile_list(key, part):
    key = jax.random.fold_in(key, 11)
    key_count, key_pick, key_ordering = jax.random.split(key, 3)
    blocks = GRID_ROW * GRID_COL
    counts = jax.random.randint(key_count, (blocks,), TILES_DEV // 4, TILE_CAP + 1)
    chosen = jax.random.randint(key_pick, (), 0, blocks)
    counts = counts.at[chosen].set(TILE_CAP)
    order_keys = jax.random.split(key_ordering, blocks)
    orders = jax.vmap(lambda one: jax.random.permutation(one, TILES_DEV))(order_keys).astype(jnp.int32)
    slots = jnp.arange(TILE_CAP, dtype=jnp.int32)
    entries = jnp.where(slots[None, :] < counts[:, None], orders[:, :TILE_CAP], TILES_DEV)
    entries = jnp.sort(entries, axis=1)
    return entries.reshape(GRID_ROW, GRID_COL, TILE_CAP).astype(jnp.int32)


def strengthened(values, stream_key, source, target, parts, factor):
    owner, partner = [(jnp.arange(values.shape[axis_at]) // (values.shape[axis_at] // parts)).reshape([-1 if axis == axis_at else 1 for axis in range(values.ndim)]) for axis_at in (source, target)]
    chosen = jax.random.permutation(stream_key, parts)[partner]
    strong = (owner == chosen) | (owner == (partner + parts // 2) % parts)
    return jnp.where(strong, factor * values, values)


def levels(stream_key, extent, pieces, low, top_value):
    loudness, own = 1.0, jax.random.fold_in(stream_key, 6)
    for axis_at, shards_of in pieces:
        heights = jnp.exp(jax.random.uniform(jax.random.fold_in(own, axis_at), (shards_of,), jnp.float32, low / len(pieces), top_value / len(pieces)))
        loudness = loudness * jnp.repeat(heights, extent[axis_at] // shards_of).reshape([-1 if axis == axis_at else 1 for axis in range(len(extent))])
    return loudness


def normal_values(rng, extent, deviation, limit, shards=(), held_as=jnp.bfloat16):
    values = jax.random.normal(rng, extent, jnp.float32) * deviation
    if len(shards) > 0:
        values = levels(rng, extent, shards, -0.22, 0.18) * values
    return jnp.clip(values, min=-limit, max=limit).astype(held_as)


def gaussian_with(stream_key, dims, width, bound, shards, heavy, held_as=jnp.bfloat16):
    values = width * jax.random.normal(stream_key, dims, jnp.float32)
    if shards:
        values = values * levels(stream_key, dims, shards, -0.22, 0.18)
    return jnp.clip(strengthened(values, jax.random.fold_in(stream_key, 3), *heavy), -bound, bound).astype(held_as)


def setup_inputs(seed: int = 0) -> dict:
    arg_keys = jax.random.split(jax.random.key(seed), 7)
    return {
        "tokens": gaussian_with(arg_keys[0], (TOKENS, MODEL_WIDTH), 1.0, 6.0, ((0, 8), (1, 16)), (1, 0, 16, 2.0)),
        "weight": normal_values(arg_keys[1], (MODEL_WIDTH, HIDDEN_WIDTH), MODEL_WIDTH ** -0.5, 0.046875, ((0, 16), (1, 8))),
        "adapter_down_matrix": normal_values(arg_keys[2], (MODEL_WIDTH, ADAPTER_RANK), MODEL_WIDTH ** -0.5, 0.046875, ((0, 16),)),
        "adapter_up_matrix": normal_values(arg_keys[3], (ADAPTER_RANK, HIDDEN_WIDTH), ADAPTER_RANK ** -0.5, 0.75, ((1, 8),)),
        "grad_out": gaussian_with(arg_keys[4], (TOKENS, HIDDEN_WIDTH), 1.0, 6.0, ((0, 16), (1, 8)), (1, 0, 16, 2.0)),
        "tile_list": draw_tile_list(jax.random.fold_in(arg_keys[6], 71), 0),
    }


def build_mask(tile_list):
    row_tiles = MODEL_WIDTH // TILE_SIDE // GRID_ROW
    col_tiles = HIDDEN_WIDTH // TILE_SIDE // GRID_COL
    numbers = jnp.arange(TILES_DEV, dtype=jnp.int32)
    hits = jnp.any(tile_list[:, :, :, None] == numbers[None, None, None, :], axis=2)
    grid = hits.reshape(GRID_ROW, GRID_COL, row_tiles, col_tiles).transpose(0, 2, 1, 3)
    grid = grid.reshape(GRID_ROW * row_tiles, GRID_COL * col_tiles)
    full = jnp.repeat(jnp.repeat(grid, TILE_SIDE, axis=0), TILE_SIDE, axis=1)
    return full.astype(jnp.bfloat16)

def reference(tokens, weight, adapter_down_matrix, adapter_up_matrix, grad_out, tile_list):
    mask = build_mask(tile_list)
    masked = weight * mask
    low = jnp.dot(tokens, adapter_down_matrix, preferred_element_type=jnp.float32)
    up_float = adapter_up_matrix.astype(jnp.float32)
    down_matrix_float = adapter_down_matrix.astype(jnp.float32)
    main = jnp.dot(tokens, masked, preferred_element_type=jnp.float32)
    projected = (main + jnp.dot(low, up_float, precision=lax.Precision.HIGHEST)).astype(jnp.bfloat16)
    grad_low = jnp.dot(grad_out, adapter_up_matrix.T, preferred_element_type=jnp.float32)
    back = jnp.dot(grad_out, masked.T, preferred_element_type=jnp.float32)
    grad_tokens = (back + jnp.dot(grad_low, down_matrix_float.T, precision=lax.Precision.HIGHEST)).astype(jnp.bfloat16)
    scale_factor = 1.0 / jnp.sqrt(jnp.float32(TOKENS))
    outer = jnp.dot(tokens.T, grad_out, preferred_element_type=jnp.float32)
    grad_weight = (outer * mask * scale_factor).astype(jnp.bfloat16)
    return (projected, grad_tokens, grad_weight)
```

```python
import functools
import math

import jax
import jax.numpy as jnp
from jax import lax
from jax.experimental import pallas as pl
from jax.experimental.pallas import tpu as pltpu
from jax.sharding import PartitionSpec as P

MESH = pl.DeviceIdType.MESH
F32 = jnp.float32
BF16 = jnp.bfloat16
TILE = 256
P_CHUNKS = ((0, 4), (4, 3), (7, 3), (10, 3))
G_CHUNKS = ((0, 1), (1, 1), (2, 1), (3, 1))
N_SEM = 96


def dot(a, b):
    return jnp.dot(a, b, preferred_element_type=F32)


def dot_t(a, b):
    return lax.dot_general(a, b, (((1,), (1,)), ((), ())), preferred_element_type=F32)


def split_terms(twice):
    first = lax.broadcasted_iota(jnp.int32, twice.shape, 1) < twice.shape[1] // 2
    high = twice.astype(BF16).astype(F32)
    rest = twice - high
    middle = rest.astype(BF16).astype(F32)
    low = rest - middle
    return (jnp.where(first, high, middle).astype(BF16), jnp.where(first, low, 0.0).astype(BF16))


def kernel(x_in, w_in, down, up, dy_in, tiles, out, gx_out, gw_out,
           x_all, dy_all, w, mask, up_ext, down_ext, x_low, dy_low, x_t, gw,
           p, p_sib, p_h1, p_h2, p_z, q, q_h1, q_h2, q_z, send, recv, local):
    r = lax.axis_index("row")
    c = lax.axis_index("col")
    core = lax.rem(r, 2)
    y, zl = r // 4, lax.rem(r // 2, 2)
    x, zh = c // 2, lax.rem(c, 2)
    rz, rs = r + 2 - 4 * zl, r + 1 - 2 * core
    rl, rr, ro = lax.rem(r + 12, 16), lax.rem(r + 4, 16), lax.rem(r + 8, 16)
    rlz, rrz, roz = lax.rem(rz + 12, 16), lax.rem(rz + 4, 16), lax.rem(rz + 8, 16)
    cz = c + 1 - 2 * zh
    cl, cr, co = lax.rem(c + 6, 8), lax.rem(c + 2, 8), lax.rem(c + 4, 8)
    clz, crz, coz = lax.rem(cz + 6, 8), lax.rem(cz + 2, 8), lax.rem(cz + 4, 8)
    sib, y_left, y_right, z_low = (rs, c), (rl, c), (rr, c), (rz, c)
    x_left, x_right, z_high = (r, cl), (r, cr), (r, cz)

    counter = [0]
    sends = []

    def ident():
        counter[0] += 1
        return counter[0] - 1

    def put(i, src, dst, device):
        copy = pltpu.make_async_remote_copy(
            src_ref=src, dst_ref=dst, send_sem=send.at[i], recv_sem=recv.at[i],
            device_id=device, device_id_type=MESH)
        copy.start()
        sends.append(copy)

    def got(i, dst):
        pltpu.make_async_remote_copy(
            src_ref=dst, dst_ref=dst, send_sem=send.at[i], recv_sem=recv.at[i],
            device_id=sib, device_id_type=MESH).wait_recv()

    w_copy = pltpu.make_async_copy(w_in, w, local.at[0])
    w_copy.start()
    x_copy = pltpu.make_async_copy(x_in, x_all.at[c], local.at[1])
    x_copy.start()
    dy_copy = pltpu.make_async_copy(dy_in, dy_all.at[r], local.at[2])
    dy_copy.start()

    barrier = pltpu.get_barrier_semaphore()
    for device in (sib, y_left, y_right, z_low, x_left, x_right, z_high):
        pl.semaphore_signal(barrier, inc=1, device_id=device, device_id_type=MESH)
    pl.semaphore_wait(barrier, 7)

    x0, x1r, x1l, x2r, x2l, x3r, x3l, x4r, x4l = (ident() for _ in range(9))
    d0, d1r, d1l, d2r, d2l, d3r, d3l, d4r, d4l = (ident() for _ in range(9))
    s = [ident() for _ in range(10)]
    put(x0, x_in, x_all.at[c], z_high)
    put(x1r, x_in, x_all.at[c], x_right)
    put(x1l, x_in, x_all.at[c], x_left)
    put(d0, dy_in, dy_all.at[r], z_low)
    put(d1r, dy_in, dy_all.at[r], y_right)
    put(d1l, dy_in, dy_all.at[r], y_left)
    put(s[0], dy_in, dy_all.at[r], sib)

    listed = tiles[...]
    number = lax.broadcasted_iota(jnp.int32, (8, listed.shape[1]), 0) * 26
    for tile in range(26):
        hit = jnp.where(jnp.broadcast_to(listed, number.shape) == number + tile, 1.0, 0.0)
        flag = jnp.sum(hit, axis=1, keepdims=True)
        mask[:, tile * 128:(tile + 1) * 128] = jnp.broadcast_to(flag, (8, 128))

    d = down[...].astype(F32)
    twice = jnp.concatenate([d, d], axis=1)
    first = lax.broadcasted_iota(jnp.int32, twice.shape, 1) < 64
    down_ext[:, :128] = twice.astype(BF16)
    down_ext[:, 128:] = jnp.where(first, twice, 0.0).astype(BF16)
    for part in range(3):
        up_ext[64 * part:64 * (part + 1), :] = up[...]
    up_ext[192:, :] = jnp.zeros_like(up)

    got(x0, x_all.at[cz])
    put(x2r, x_all.at[cz], x_all.at[cz], x_right)
    put(x2l, x_all.at[cz], x_all.at[cz], x_left)
    got(x1r, x_all.at[cl])
    put(x3r, x_all.at[cl, 0], x_all.at[cl, 0], x_right)
    got(x1l, x_all.at[cr])
    put(x3l, x_all.at[cr, 1], x_all.at[cr, 1], x_left)

    w_copy.wait()

    def masking(step, carry):
        at = pl.ds(pl.multiple_of(step * TILE, TILE), TILE)
        for block in range(8):
            rows = slice(block * 128, (block + 1) * 128)
            keep = mask[block:block + 1, at].astype(BF16)
            w[rows, at] = w[rows, at] * jnp.broadcast_to(keep, (128, TILE))
        return carry

    lax.fori_loop(0, 13, masking, 0)

    got(d0, dy_all.at[rz])
    put(d2r, dy_all.at[rz], dy_all.at[rz], y_right)
    put(d2l, dy_all.at[rz], dy_all.at[rz], y_left)
    put(s[1], dy_all.at[rz], dy_all.at[rz], sib)
    got(x2r, x_all.at[clz])
    put(x4r, x_all.at[clz, 0], x_all.at[clz, 0], x_right)
    got(x2l, x_all.at[crz])
    put(x4l, x_all.at[crz, 1], x_all.at[crz, 1], x_left)
    got(d1r, dy_all.at[rl])
    put(d3r, dy_all.at[rl, 0], dy_all.at[rl, 0], y_right)
    put(s[2], dy_all.at[rl], dy_all.at[rl], sib)
    got(d1l, dy_all.at[rr])
    put(d3l, dy_all.at[rr, 1], dy_all.at[rr, 1], y_left)
    put(s[3], dy_all.at[rr], dy_all.at[rr], sib)
    got(x3r, x_all.at[co, 0])
    got(x3l, x_all.at[co, 1])
    got(x4r, x_all.at[coz, 0])
    got(x4l, x_all.at[coz, 1])
    x_copy.wait()

    def x_rows():
        return x_all[...].reshape(512, 1024)

    parts = split_terms(dot(x_rows(), down_ext[:, :128]))
    x_low[:, :128] = parts[0]
    x_low[:, 128:] = parts[1]

    p_ids = [[ident() for _ in range(5)] for _ in P_CHUNKS]
    q_ids = [[ident() for _ in range(5)] for _ in G_CHUNKS]

    def span(chunk):
        return slice(chunk[0] * TILE, (chunk[0] + chunk[1]) * TILE)

    def p_compute(n):
        def step(i, carry):
            at = pl.ds(pl.multiple_of(i * TILE, TILE), TILE)
            value = dot(x_rows(), w[:, at]) + dot(x_low[...], up_ext[:, at])
            p[:, :, :, :, at] = value.reshape(4, 2, 2, 32, TILE)
            return carry

        first, count = P_CHUNKS[n]
        lax.fori_loop(first, first + count, step, 0)
        at = span(P_CHUNKS[n])
        put(p_ids[n][0], p.at[:, :, 1 - core, :, at], p_sib.at[:, :, :, at], sib)

    def p_pair(n):
        at = span(P_CHUNKS[n])
        got(p_ids[n][0], p_sib.at[:, :, :, at])
        p[:, :, core, :, at] = p[:, :, core, :, at] + p_sib[:, :, :, at]
        first_hop(n, p_ids[n], lambda k: p.at[k, :, core, :, at], p_h1.at[:, :, at], p_h2.at[:, :, :, at], y, y_left, y_right)

    def first_hop(n, ids, view, h1, h2, k, left, right):
        far, lower, upper = lax.rem(k + 2, 4), lax.rem(k + 3, 4), lax.rem(k + 1, 4)
        if n % 2 == 0:
            put(ids[1], view(far), h1, left)
            put(ids[3], view(upper), h2.at[1], right)
        else:
            put(ids[1], view(far), h1, right)
            put(ids[2], view(lower), h2.at[0], left)

    def second_hop(n, ids, view, h1, h2, k, left, right):
        lower, upper = lax.rem(k + 3, 4), lax.rem(k + 1, 4)
        got(ids[1], h1)
        target = view(lower) if n % 2 == 0 else view(upper)
        target[...] = target[...] + h1[...]
        if n % 2 == 0:
            put(ids[2], target, h2.at[0], left)
        else:
            put(ids[3], target, h2.at[1], right)

    def third_hop(n, ids, view, h2, z, k, other, device):
        got(ids[2], h2.at[0])
        got(ids[3], h2.at[1])
        total = view(k)
        total[...] = total[...] + h2[0] + h2[1]
        put(ids[4], total.at[other], z, device)

    def p_second(n):
        at = span(P_CHUNKS[n])
        second_hop(n, p_ids[n], lambda k: p.at[k, :, core, :, at], p_h1.at[:, :, at], p_h2.at[:, :, :, at], y, y_left, y_right)

    def p_third(n):
        at = span(P_CHUNKS[n])
        third_hop(n, p_ids[n], lambda k: p.at[k, :, core, :, at], p_h2.at[:, :, :, at], p_z.at[:, at], y, 1 - zl, z_low)

    def p_last(n):
        at = span(P_CHUNKS[n])
        got(p_ids[n][4], p_z.at[:, at])
        out[:, at] = (p[y, zl, core, :, at] + p_z[:, at]).astype(BF16)

    def q_compute(n):
        at = span(G_CHUNKS[n])
        value = dot_t(dy_all[...].reshape(512, 3328), w[at, :]) + dot_t(dy_low[...], down_ext[at, :])
        q[:, :, :, at] = value.reshape(4, 2, 64, value.shape[1])
        first_hop(n, q_ids[n], lambda k: q.at[k, :, :, at], q_h1.at[:, :, at], q_h2.at[:, :, :, at], x, x_left, x_right)

    def q_second(n):
        at = span(G_CHUNKS[n])
        second_hop(n, q_ids[n], lambda k: q.at[k, :, :, at], q_h1.at[:, :, at], q_h2.at[:, :, :, at], x, x_left, x_right)

    def q_third(n):
        at = span(G_CHUNKS[n])
        third_hop(n, q_ids[n], lambda k: q.at[k, :, :, at], q_h2.at[:, :, :, at], q_z.at[:, at], x, 1 - zh, z_high)

    def q_last(n):
        at = span(G_CHUNKS[n])
        got(q_ids[n][4], q_z.at[:, at])
        gx_out[:, at] = (q[x, zh, :, at] + q_z[:, at]).astype(BF16)

    gw_copies = []

    def gw_compute(first, last):
        def step(i, carry):
            at = pl.ds(pl.multiple_of(i * TILE, TILE), TILE)
            for half in range(2):
                rows = slice(half * 512, (half + 1) * 512)
                value = dot(x_t[rows, :], dy_all[:, :, :, at].reshape(512, TILE))
                for block in range(4):
                    keep = mask[half * 4 + block:half * 4 + block + 1, at] * (1.0 / math.sqrt(512))
                    gw[half * 512 + block * 128:half * 512 + (block + 1) * 128, at] = (
                        value[block * 128:(block + 1) * 128] * keep).astype(BF16)
            return carry

        lax.fori_loop(first, last, step, 0)
        at = slice(first * TILE, last * TILE)
        copy = pltpu.make_async_copy(gw.at[:, at], gw_out.at[:, at], local.at[3 + len(gw_copies)])
        copy.start()
        gw_copies.append(copy)

    p_compute(0)
    p_compute(1)
    p_pair(0)
    got(d2r, dy_all.at[rlz])
    put(d4r, dy_all.at[rlz, 0], dy_all.at[rlz, 0], y_right)
    put(s[4], dy_all.at[rlz], dy_all.at[rlz], sib)
    got(d2l, dy_all.at[rrz])
    put(d4l, dy_all.at[rrz, 1], dy_all.at[rrz, 1], y_left)
    put(s[5], dy_all.at[rrz], dy_all.at[rrz], sib)
    p_compute(2)
    p_pair(1)
    got(d3r, dy_all.at[ro, 0])
    put(s[6], dy_all.at[ro, 0], dy_all.at[ro, 0], sib)
    got(d3l, dy_all.at[ro, 1])
    put(s[7], dy_all.at[ro, 1], dy_all.at[ro, 1], sib)
    p_compute(3)
    p_pair(2)
    for quarter in range(4):
        cols = slice(quarter * 256, (quarter + 1) * 256)
        x_t[cols, :] = x_all[:, :, :, cols].reshape(512, 256).T
    p_pair(3)
    got(d4r, dy_all.at[roz, 0])
    put(s[8], dy_all.at[roz, 0], dy_all.at[roz, 0], sib)
    got(d4l, dy_all.at[roz, 1])
    put(s[9], dy_all.at[roz, 1], dy_all.at[roz, 1], sib)

    dy_copy.wait()
    for i, index in enumerate((r, rz, rl, rr, rlz, rrz)):
        got(s[i], dy_all.at[index + 1 - 2 * core])
    for i, index in enumerate((ro, roz)):
        for half in range(2):
            got(s[6 + 2 * i + half], dy_all.at[index + 1 - 2 * core, half])

    parts = split_terms(dot_t(dy_all[...].reshape(512, 3328), up_ext[:128, :]))
    dy_low[:, :128] = parts[0]
    dy_low[:, 128:] = parts[1]

    q_compute(0)
    p_second(0)
    q_compute(1)
    p_second(1)
    q_second(0)
    q_compute(2)
    p_second(2)
    q_second(1)
    q_compute(3)
    p_second(3)
    q_second(2)
    gw_compute(0, 3)
    p_third(0)
    q_second(3)
    gw_compute(3, 6)
    q_third(0)
    p_third(1)
    gw_compute(6, 9)
    q_third(1)
    p_third(2)
    gw_compute(9, 11)
    q_third(2)
    gw_compute(11, 13)
    q_third(3)
    for n in range(4):
        q_last(n)
    p_third(3)
    for n in range(4):
        p_last(n)
    for copy in gw_copies:
        copy.wait()
    for copy in sends:
        copy.wait_send()


def body(tokens, weight, down, up, grad_out, tile_list):
    anywhere = pl.BlockSpec(memory_space=pl.ANY)
    vmem = pl.BlockSpec(memory_space=pltpu.VMEM)
    scratch = [
        pltpu.VMEM((8, 2, 32, 1024), BF16),
        pltpu.VMEM((16, 2, 16, 3328), BF16),
        pltpu.VMEM((1024, 3328), BF16),
        pltpu.VMEM((8, 3328), F32),
        pltpu.VMEM((256, 3328), BF16),
        pltpu.VMEM((1024, 256), BF16),
        pltpu.VMEM((512, 256), BF16),
        pltpu.VMEM((512, 256), BF16),
        pltpu.VMEM((1024, 512), BF16),
        pltpu.VMEM((1024, 3328), BF16),
        pltpu.VMEM((4, 2, 2, 32, 3328), F32),
        pltpu.VMEM((4, 2, 32, 3328), F32),
        pltpu.VMEM((2, 32, 3328), F32),
        pltpu.VMEM((2, 2, 32, 3328), F32),
        pltpu.VMEM((32, 3328), F32),
        pltpu.VMEM((4, 2, 64, 1024), F32),
        pltpu.VMEM((2, 64, 1024), F32),
        pltpu.VMEM((2, 2, 64, 1024), F32),
        pltpu.VMEM((64, 1024), F32),
        pltpu.SemaphoreType.DMA((N_SEM,)),
        pltpu.SemaphoreType.DMA((N_SEM,)),
        pltpu.SemaphoreType.DMA((8,)),
    ]
    return pl.pallas_call(
        kernel,
        out_shape=(
            jax.ShapeDtypeStruct((32, 3328), BF16),
            jax.ShapeDtypeStruct((64, 1024), BF16),
            jax.ShapeDtypeStruct((1024, 3328), BF16),
        ),
        in_specs=[anywhere, anywhere, vmem, vmem, anywhere, vmem],
        out_specs=(vmem, vmem, anywhere),
        scratch_shapes=scratch,
        compiler_params=pltpu.CompilerParams(
            collective_id=0, has_side_effects=True, vmem_limit_bytes=60 * 2**20),
        cost_estimate=pl.CostEstimate(flops=3 * 2 * 512 * 1024 * 3328, bytes_accessed=14 * 2**20, transcendentals=0),
    )(tokens.reshape(2, 32, 1024), weight, down, up, grad_out.reshape(2, 16, 3328), tile_list.reshape(1, -1))


def solution(mesh):
    return jax.shard_map(
        body,
        mesh=mesh,
        in_specs=(
            P("col", "row"),
            P("row", "col"),
            P("row", None),
            P(None, "col"),
            P("row", "col"),
            P("row", "col", None),
        ),
        out_specs=(P("row", "col"), P("col", "row"), P("row", "col")),
        check_vma=False,
    )
```

```python
import functools
import math

import jax
import jax.numpy as jnp
from jax import lax
from jax.experimental import pallas as pl
from jax.experimental.pallas import tpu as pltpu
from jax.sharding import PartitionSpec as P

MESH = pl.DeviceIdType.MESH
F32 = jnp.float32
BF16 = jnp.bfloat16
I16 = jnp.int16
TILE = 256
P_CHUNKS = ((0, 4), (4, 3), (7, 3), (10, 3))
G_CHUNKS = ((0, 1), (1, 1), (2, 1), (3, 1))
N_SEM = 96


def dot(a, b):
    return jnp.dot(a, b, preferred_element_type=F32)


def dot_t(a, b):
    return lax.dot_general(a, b, (((1,), (1,)), ((), ())), preferred_element_type=F32)


def split_terms(twice):
    first = lax.broadcasted_iota(jnp.int32, twice.shape, 1) < twice.shape[1] // 2
    high = twice.astype(BF16).astype(F32)
    rest = twice - high
    middle = rest.astype(BF16).astype(F32)
    low = rest - middle
    return (jnp.where(first, high, middle).astype(BF16), jnp.where(first, low, 0.0).astype(BF16))


def diagonal(rows):
    shape = (rows, 128)
    return lax.broadcasted_iota(jnp.int32, shape, 0) == lax.broadcasted_iota(jnp.int32, shape, 1)


def encode(value, code, scale):
    value = value.reshape(code.shape)
    top = jnp.maximum(jnp.max(jnp.abs(value), axis=1, keepdims=True), 1e-30)
    code[...] = jnp.round(value * (32760.0 / top)).astype(jnp.int32).astype(jnp.int16)
    row = jnp.sum(jnp.where(diagonal(code.shape[0]), top * (1.0 / 32760.0), 0.0), axis=0, keepdims=True)
    scale[...] = jnp.broadcast_to(row, (8, 128))


def decode(code, scale, shape):
    rows = code.shape[0]
    row = jnp.broadcast_to(scale[0:1, :], (rows, 128))
    column = jnp.sum(jnp.where(diagonal(rows), row, 0.0), axis=1, keepdims=True)
    return (code[...].astype(jnp.int32).astype(F32) * column).reshape(shape)


def kernel(x_in, w_in, down_in, up_in, dy_in, tiles_in, out, gx_out, gw,
           x_all, dy_all, w, tiles, mask, up_ext, down_ext, x_low, dy_low, x_t,
           p, p_sib, p_out, p_in, pz_out, pz_in, q, q_out, q_in, qz_out, qz_in, scale_out, scale_in, send, recv, local):
    r = lax.axis_index("row")
    c = lax.axis_index("col")
    core = lax.rem(r, 2)
    y, zl = r // 4, lax.rem(r // 2, 2)
    x, zh = c // 2, lax.rem(c, 2)
    rz, rs = r + 2 - 4 * zl, r + 1 - 2 * core
    rl, rr, ro = lax.rem(r + 12, 16), lax.rem(r + 4, 16), lax.rem(r + 8, 16)
    rlz, rrz, roz = lax.rem(rz + 12, 16), lax.rem(rz + 4, 16), lax.rem(rz + 8, 16)
    cz = c + 1 - 2 * zh
    cl, cr, co = lax.rem(c + 6, 8), lax.rem(c + 2, 8), lax.rem(c + 4, 8)
    clz, crz, coz = lax.rem(cz + 6, 8), lax.rem(cz + 2, 8), lax.rem(cz + 4, 8)
    sib, y_left, y_right, z_low = (rs, c), (rl, c), (rr, c), (rz, c)
    x_left, x_right, z_high = (r, cl), (r, cr), (r, cz)

    counter = [0]
    sends = []

    def ident():
        counter[0] += 1
        return counter[0] - 1

    def put(i, src, dst, device):
        copy = pltpu.make_async_remote_copy(
            src_ref=src, dst_ref=dst, send_sem=send.at[i], recv_sem=recv.at[i],
            device_id=device, device_id_type=MESH)
        copy.start()
        sends.append(copy)

    def got(i, dst):
        pltpu.make_async_remote_copy(
            src_ref=dst, dst_ref=dst, send_sem=send.at[i], recv_sem=recv.at[i],
            device_id=sib, device_id_type=MESH).wait_recv()

    w_copy = pltpu.make_async_copy(w_in, w, local.at[0])
    w_copy.start()
    x_copy = pltpu.make_async_copy(x_in, x_all.at[c], local.at[1])
    x_copy.start()
    dy_copy = pltpu.make_async_copy(dy_in, dy_all.at[r], local.at[2])
    dy_copy.start()

    small = [pltpu.make_async_copy(tiles_in, tiles, local.at[3])]
    for part in range(3):
        rows = slice(64 * part, 64 * (part + 1))
        small.append(pltpu.make_async_copy(down_in, down_ext.at[rows], local.at[4 + part]))
        small.append(pltpu.make_async_copy(up_in, up_ext.at[rows], local.at[7 + part]))
    for copy in small:
        copy.start()

    barrier = pltpu.get_barrier_semaphore()
    for device in (sib, y_left, y_right, z_low, x_left, x_right, z_high):
        pl.semaphore_signal(barrier, inc=1, device_id=device, device_id_type=MESH)
    pl.semaphore_wait(barrier, 7)

    x0, x1r, x1l, x2r, x2l, x3r, x3l, x4r, x4l = (ident() for _ in range(9))
    d0, d1r, d1l, d2r, d2l, d3r, d3l, d4r, d4l = (ident() for _ in range(9))
    s = [ident() for _ in range(10)]
    put(x0, x_in, x_all.at[c], z_high)
    put(x1r, x_in, x_all.at[c], x_right)
    put(x1l, x_in, x_all.at[c], x_left)
    put(d1r, dy_in, dy_all.at[r], y_right)
    put(d1l, dy_in, dy_all.at[r], y_left)
    put(s[0], dy_in, dy_all.at[r], sib)

    small[0].wait()
    listed = tiles[...]
    number = lax.broadcasted_iota(jnp.int32, (8, listed.shape[1]), 0) * 26
    for tile in range(26):
        hit = jnp.where(jnp.broadcast_to(listed, number.shape) == number + tile, 1.0, 0.0)
        flag = jnp.sum(hit, axis=1, keepdims=True)
        mask[:, tile * 128:(tile + 1) * 128] = jnp.broadcast_to(flag, (8, 128))

    down_ext[192:, :] = jnp.zeros((64, 1024), BF16)
    up_ext[192:, :] = jnp.zeros((64, 3328), BF16)
    for copy in small[1:]:
        copy.wait()

    got(x0, x_all.at[cz])
    put(x2r, x_all.at[cz], x_all.at[cz], x_right)
    put(x2l, x_all.at[cz], x_all.at[cz], x_left)
    put(d0, dy_in, dy_all.at[r], z_low)
    got(x1r, x_all.at[cl])
    put(x3r, x_all.at[cl, 0], x_all.at[cl, 0], x_right)
    got(x1l, x_all.at[cr])
    put(x3l, x_all.at[cr, 1], x_all.at[cr, 1], x_left)

    got(d1r, dy_all.at[rl])
    put(d3r, dy_all.at[rl, 0], dy_all.at[rl, 0], y_right)
    put(s[2], dy_all.at[rl], dy_all.at[rl], sib)
    got(d1l, dy_all.at[rr])
    put(d3l, dy_all.at[rr, 1], dy_all.at[rr, 1], y_left)
    put(s[3], dy_all.at[rr], dy_all.at[rr], sib)
    got(x2r, x_all.at[clz])
    put(x4r, x_all.at[clz, 0], x_all.at[clz, 0], x_right)
    got(x2l, x_all.at[crz])
    put(x4l, x_all.at[crz, 1], x_all.at[crz, 1], x_left)

    w_copy.wait()

    def masking(step, carry):
        at = pl.ds(pl.multiple_of(step * TILE, TILE), TILE)
        for block in range(8):
            rows = slice(block * 128, (block + 1) * 128)
            keep = mask[block:block + 1, at].astype(BF16)
            w[rows, at] = w[rows, at] * jnp.broadcast_to(keep, (128, TILE))
        return carry

    lax.fori_loop(0, 13, masking, 0)

    got(d0, dy_all.at[rz])
    put(d2r, dy_all.at[rz], dy_all.at[rz], y_right)
    put(d2l, dy_all.at[rz], dy_all.at[rz], y_left)
    put(s[1], dy_all.at[rz], dy_all.at[rz], sib)
    got(x3r, x_all.at[co, 0])
    got(x3l, x_all.at[co, 1])
    got(x4r, x_all.at[coz, 0])
    got(x4l, x_all.at[coz, 1])
    x_copy.wait()

    def x_rows():
        return x_all[...].reshape(512, 1024)

    parts = split_terms(dot_t(x_rows(), down_ext[:128, :]))
    x_low[:, :128] = parts[0]
    x_low[:, 128:] = parts[1]

    p_sib_ids = [ident() for _ in P_CHUNKS]

    def span(chunk):
        return slice(chunk[0] * TILE, (chunk[0] + chunk[1]) * TILE)

    def p_compute(n):
        def step(i, carry):
            at = pl.ds(pl.multiple_of(i * TILE, TILE), TILE)
            value = dot(x_rows(), w[:, at]) + dot(x_low[...], up_ext[:, at])
            p[:, :, :, :, at] = value.reshape(4, 2, 2, 32, TILE)
            return carry

        first, count = P_CHUNKS[n]
        lax.fori_loop(first, first + count, step, 0)
        at = span(P_CHUNKS[n])
        put(p_sib_ids[n], p.at[:, :, 1 - core, :, at], p_sib.at[:, :, :, at], sib)

    def ring_sum(chunks, view, shape, out_codes, in_codes, z_out, z_in, k, other, left, right, z_device, finish):
        far, lower, upper = lax.rem(k + 2, 4), lax.rem(k + 3, 4), lax.rem(k + 1, 4)
        ids = [[(ident(), ident(), scale_id()) for _ in range(4)] for _ in chunks]

        def post(n, hop, value, code_out, code_in, device):
            data, scales, slot = ids[n][hop]
            encode(value, code_out, scale_out.at[slot])
            put(data, code_out, code_in, device)
            put(scales, scale_out.at[slot], scale_in.at[slot], device)

        def take(n, hop, code_in, to):
            data, scales, slot = ids[n][hop]
            got(data, code_in)
            got(scales, scale_in.at[slot])
            return decode(code_in, scale_in.at[slot], to)

        def block(n):
            at = span(chunks[n])
            return at, shape + (at.stop - at.start,)

        def first(n):
            at, _ = block(n)
            post(n, 0, view(far, at)[...], out_codes.at[0, :, at], in_codes.at[0, :, at], (left, right)[n % 2])
            if n % 2 == 0:
                post(n, 2, view(upper, at)[...], out_codes.at[2, :, at], in_codes.at[2, :, at], right)
            else:
                post(n, 1, view(lower, at)[...], out_codes.at[1, :, at], in_codes.at[1, :, at], left)

        def second(n):
            at, to = block(n)
            came = take(n, 0, in_codes.at[0, :, at], to)
            if n % 2 == 0:
                post(n, 1, view(lower, at)[...] + came, out_codes.at[1, :, at], in_codes.at[1, :, at], left)
            else:
                post(n, 2, view(upper, at)[...] + came, out_codes.at[2, :, at], in_codes.at[2, :, at], right)

        def third(n):
            at, to = block(n)
            total = view(k, at)
            total[...] = (total[...] + take(n, 1, in_codes.at[1, :, at], to)
                          + take(n, 2, in_codes.at[2, :, at], to))
            post(n, 3, total[other], z_out.at[:, at], z_in.at[:, at], z_device)

        def last(n):
            at, to = block(n)
            finish(at, view(k, at)[1 - other] + take(n, 3, z_in.at[:, at], to[1:]))

        return first, second, third, last

    scale_counter = [0]

    def scale_id():
        scale_counter[0] += 1
        return scale_counter[0] - 1

    def p_view(k, at):
        return p.at[k, :, core, :, at]

    def p_finish(at, value):
        out[:, at] = value.astype(BF16)

    def q_view(k, at):
        return q.at[k, :, :, at]

    def q_finish(at, value):
        gx_out[:, at] = value.astype(BF16)

    p_first, p_second, p_third, p_last = ring_sum(
        P_CHUNKS, p_view, (2, 32), p_out, p_in, pz_out, pz_in, y, 1 - zl, y_left, y_right, z_low, p_finish)
    q_first, q_second, q_third, q_last = ring_sum(
        G_CHUNKS, q_view, (2, 64), q_out, q_in, qz_out, qz_in, x, 1 - zh, x_left, x_right, z_high, q_finish)

    def p_pair(n):
        at = span(P_CHUNKS[n])
        got(p_sib_ids[n], p_sib.at[:, :, :, at])
        p[:, :, core, :, at] = p[:, :, core, :, at] + p_sib[:, :, :, at]
        p_first(n)

    def q_compute(n):
        at = span(G_CHUNKS[n])
        value = dot_t(dy_all[...].reshape(512, 3328), w[at, :]) + dot(dy_low[...], down_ext[:, at])
        q[:, :, :, at] = value.reshape(4, 2, 64, value.shape[1])
        q_first(n)

    def gw_compute(first, last):
        def step(i, carry):
            at = pl.ds(pl.multiple_of(i * TILE, TILE), TILE)
            for half in range(2):
                rows = slice(half * 512, (half + 1) * 512)
                value = dot(x_t[rows, :], dy_all[:, :, :, at].reshape(512, TILE))
                for block in range(4):
                    keep = mask[half * 4 + block:half * 4 + block + 1, at] * (1.0 / math.sqrt(512))
                    gw[half * 512 + block * 128:half * 512 + (block + 1) * 128, at] = (
                        value[block * 128:(block + 1) * 128] * keep).astype(BF16)
            return carry

        lax.fori_loop(first, last, step, 0)

    p_compute(0)
    p_compute(1)
    p_pair(0)
    got(d2r, dy_all.at[rlz])
    put(d4r, dy_all.at[rlz, 0], dy_all.at[rlz, 0], y_right)
    put(s[4], dy_all.at[rlz], dy_all.at[rlz], sib)
    got(d2l, dy_all.at[rrz])
    put(d4l, dy_all.at[rrz, 1], dy_all.at[rrz, 1], y_left)
    put(s[5], dy_all.at[rrz], dy_all.at[rrz], sib)
    p_compute(2)
    p_pair(1)
    got(d3r, dy_all.at[ro, 0])
    put(s[6], dy_all.at[ro, 0], dy_all.at[ro, 0], sib)
    got(d3l, dy_all.at[ro, 1])
    put(s[7], dy_all.at[ro, 1], dy_all.at[ro, 1], sib)
    p_compute(3)
    p_pair(2)
    for quarter in range(4):
        cols = slice(quarter * 256, (quarter + 1) * 256)
        x_t[cols, :] = x_all[:, :, :, cols].reshape(512, 256).T
    p_pair(3)
    got(d4r, dy_all.at[roz, 0])
    put(s[8], dy_all.at[roz, 0], dy_all.at[roz, 0], sib)
    got(d4l, dy_all.at[roz, 1])
    put(s[9], dy_all.at[roz, 1], dy_all.at[roz, 1], sib)

    dy_copy.wait()
    for i, index in enumerate((r, rz, rl, rr, rlz, rrz)):
        got(s[i], dy_all.at[index + 1 - 2 * core])
    for i, index in enumerate((ro, roz)):
        for half in range(2):
            got(s[6 + 2 * i + half], dy_all.at[index + 1 - 2 * core, half])

    parts = split_terms(dot_t(dy_all[...].reshape(512, 3328), up_ext[:128, :]))
    dy_low[:, :128] = parts[0]
    dy_low[:, 128:] = parts[1]

    q_compute(0)
    p_second(0)
    q_compute(1)
    p_second(1)
    q_second(0)
    q_compute(2)
    p_second(2)
    q_second(1)
    q_compute(3)
    p_second(3)
    q_second(2)
    gw_compute(0, 3)
    p_third(0)
    q_second(3)
    gw_compute(3, 6)
    q_third(0)
    p_third(1)
    gw_compute(6, 9)
    q_third(1)
    p_third(2)
    gw_compute(9, 11)
    q_third(2)
    gw_compute(11, 13)
    q_third(3)
    for n in range(4):
        q_last(n)
    p_third(3)
    for n in range(4):
        p_last(n)
    for copy in sends:
        copy.wait_send()


def store(out, gx, gw, out_to, gx_to, gw_to, sems):
    pairs = [(gw.at[pl.ds(128 * i, 128)], gw_to.at[pl.ds(128 * i, 128)]) for i in range(8)]
    pairs += [(out, out_to), (gx, gx_to)]
    copies = [pltpu.make_async_copy(src, dst, sems.at[i]) for i, (src, dst) in enumerate(pairs)]
    for copy in copies:
        copy.start()
    for copy in copies:
        copy.wait()


def body(tokens, weight, down, up, grad_out, tile_list):
    anywhere = pl.BlockSpec(memory_space=pl.ANY)
    vmem = pl.BlockSpec(memory_space=pltpu.VMEM)
    scratch = [
        pltpu.VMEM((8, 2, 32, 1024), BF16),
        pltpu.VMEM((16, 2, 16, 3328), BF16),
        pltpu.VMEM((1024, 3328), BF16),
        pltpu.VMEM((1, 156), jnp.int32),
        pltpu.VMEM((8, 3328), F32),
        pltpu.VMEM((256, 3328), BF16),
        pltpu.VMEM((256, 1024), BF16),
        pltpu.VMEM((512, 256), BF16),
        pltpu.VMEM((512, 256), BF16),
        pltpu.VMEM((1024, 512), BF16),
        pltpu.VMEM((4, 2, 2, 32, 3328), F32),
        pltpu.VMEM((4, 2, 32, 3328), F32),
        pltpu.VMEM((3, 64, 3328), I16),
        pltpu.VMEM((3, 64, 3328), I16),
        pltpu.VMEM((32, 3328), I16),
        pltpu.VMEM((32, 3328), I16),
        pltpu.VMEM((4, 2, 64, 1024), F32),
        pltpu.VMEM((3, 128, 1024), I16),
        pltpu.VMEM((3, 128, 1024), I16),
        pltpu.VMEM((64, 1024), I16),
        pltpu.VMEM((64, 1024), I16),
        pltpu.VMEM((32, 8, 128), F32),
        pltpu.VMEM((32, 8, 128), F32),
        pltpu.SemaphoreType.DMA((N_SEM,)),
        pltpu.SemaphoreType.DMA((N_SEM,)),
        pltpu.SemaphoreType.DMA((10,)),
    ]
    shapes = ((32, 3328), (64, 1024), (1024, 3328))
    results = pl.pallas_call(
        kernel,
        out_shape=tuple(pltpu.VMEM(shape, BF16) for shape in shapes),
        in_specs=[pl.BlockSpec(memory_space=pltpu.HBM)] * 6,
        out_specs=(vmem, vmem, vmem),
        scratch_shapes=scratch,
        compiler_params=pltpu.CompilerParams(
            collective_id=0, has_side_effects=True, vmem_limit_bytes=57 * 2**20),
        cost_estimate=pl.CostEstimate(flops=3 * 2 * 512 * 1024 * 3328, bytes_accessed=14 * 2**20, transcendentals=0),
    )(tokens.reshape(2, 32, 1024), weight, down.T, up, grad_out.reshape(2, 16, 3328), tile_list.reshape(1, -1))
    return pl.pallas_call(
        store,
        out_shape=tuple(jax.ShapeDtypeStruct(shape, BF16) for shape in shapes),
        in_specs=[vmem] * 3,
        out_specs=(anywhere,) * 3,
        scratch_shapes=[pltpu.SemaphoreType.DMA((10,))],
        compiler_params=pltpu.CompilerParams(vmem_limit_bytes=2**20),
        cost_estimate=pl.CostEstimate(flops=0, bytes_accessed=8 * 2**20, transcendentals=0),
    )(*results)


def solution(mesh):
    return jax.shard_map(
        body,
        mesh=mesh,
        in_specs=(
            P("col", "row"),
            P("row", "col"),
            P("row", None),
            P(None, "col"),
            P("row", "col"),
            P("row", "col", None),
        ),
        out_specs=(P("row", "col"), P("col", "row"), P("row", "col")),
        check_vma=False,
    )
```

```python
import functools
import math

import jax
import jax.numpy as jnp
from jax import lax
from jax.experimental import pallas as pl
from jax.experimental.pallas import tpu as pltpu
from jax.sharding import PartitionSpec as P

MESH = pl.DeviceIdType.MESH
F32 = jnp.float32
BF16 = jnp.bfloat16
I16 = jnp.int16
TILE = 256
P_CHUNKS = ((0, 7), (7, 6))
G_CHUNKS = ((0, 2), (2, 2))
P_DIRECT, Q_DIRECT = False, True
N_SEM = 128


def dot(a, b):
    return jnp.dot(a, b, preferred_element_type=F32)


def dot_t(a, b):
    return lax.dot_general(a, b, (((1,), (1,)), ((), ())), preferred_element_type=F32)


def split_terms(twice):
    first = lax.broadcasted_iota(jnp.int32, twice.shape, 1) < twice.shape[1] // 2
    high = twice.astype(BF16).astype(F32)
    rest = twice - high
    middle = rest.astype(BF16).astype(F32)
    low = rest - middle
    return (jnp.where(first, high, middle).astype(BF16), jnp.where(first, low, 0.0).astype(BF16))


def diagonal(rows):
    shape = (rows, 128)
    return lax.broadcasted_iota(jnp.int32, shape, 0) == lax.broadcasted_iota(jnp.int32, shape, 1)


def encode(value, code, scale):
    top = jnp.maximum(jnp.max(jnp.abs(value), axis=1, keepdims=True), 1e-30)
    code[...] = jnp.round(value * (32760.0 / top)).astype(jnp.int32).astype(jnp.int16)
    row = jnp.sum(jnp.where(diagonal(code.shape[0]), top * (1.0 / 32760.0), 0.0), axis=0, keepdims=True)
    scale[...] = jnp.broadcast_to(row, (8, 128))


def decode(code, scale):
    rows = code.shape[0]
    row = jnp.broadcast_to(scale[0:1, :], (rows, 128))
    column = jnp.sum(jnp.where(diagonal(rows), row, 0.0), axis=1, keepdims=True)
    return code[...].astype(jnp.int32).astype(F32) * column


def kernel(x_in, w_in, down_in, up_in, dy_in, tiles_in, out, gx_out, gw,
           x_all, dy_all, w, tiles, mask, up_ext, down_ext, x_low, dy_low, x_t,
           p, p_sib, p_out, p_in, pz_out, pz_in, q, q_out, q_in, qz_out, qz_in, scale_out, scale_in, send, recv, local):
    r = lax.axis_index("row")
    c = lax.axis_index("col")
    core = lax.rem(r, 2)
    y, zl = r // 4, lax.rem(r // 2, 2)
    x, zh = c // 2, lax.rem(c, 2)
    other, zlo, zho = 1 - core, 1 - zl, 1 - zh
    yl, yr, yo = lax.rem(y + 3, 4), lax.rem(y + 1, 4), lax.rem(y + 2, 4)
    xl, xr, xo = lax.rem(x + 3, 4), lax.rem(x + 1, 4), lax.rem(x + 2, 4)
    sib, z_low, z_high = (r + 1 - 2 * core, c), (r + 2 - 4 * zl, c), (r, c + 1 - 2 * zh)
    y_left, y_right = (lax.rem(r + 12, 16), c), (lax.rem(r + 4, 16), c)
    x_left, x_right = (r, lax.rem(c + 6, 8)), (r, lax.rem(c + 2, 8))
    y_far, x_far = (lax.rem(r + 8, 16), c), (r, lax.rem(c + 4, 8))

    counter = [0]
    sends = []

    def ident():
        counter[0] += 1
        return counter[0] - 1

    scale_counter = [0]

    def scale_id():
        scale_counter[0] += 1
        return scale_counter[0] - 1

    def put(i, src, dst, device):
        copy = pltpu.make_async_remote_copy(
            src_ref=src, dst_ref=dst, send_sem=send.at[i], recv_sem=recv.at[i],
            device_id=device, device_id_type=MESH)
        copy.start()
        sends.append(copy)

    def relay(i, ref, device):
        put(i, ref, ref, device)

    def got(i, dst):
        pltpu.make_async_remote_copy(
            src_ref=dst, dst_ref=dst, send_sem=send.at[i], recv_sem=recv.at[i],
            device_id=sib, device_id_type=MESH).wait_recv()

    w_copy = pltpu.make_async_copy(w_in, w, local.at[0])
    w_copy.start()
    x_copy = pltpu.make_async_copy(x_in, x_all.at[x, zh], local.at[1])
    x_copy.start()
    dy_copy = pltpu.make_async_copy(dy_in, dy_all.at[y, zl, core], local.at[2])
    dy_copy.start()
    small = [pltpu.make_async_copy(tiles_in, tiles, local.at[3])]
    for part in range(3):
        rows = slice(64 * part, 64 * (part + 1))
        small.append(pltpu.make_async_copy(down_in, down_ext.at[rows], local.at[4 + part]))
        small.append(pltpu.make_async_copy(up_in, up_ext.at[rows], local.at[7 + part]))
    for copy in small:
        copy.start()

    barrier = pltpu.get_barrier_semaphore()
    partners = [sib, y_left, y_right, z_low, x_left, x_right, z_high]
    partners += [y_far] * P_DIRECT + [x_far] * Q_DIRECT
    for device in partners:
        pl.semaphore_signal(barrier, inc=1, device_id=device, device_id_type=MESH)
    pl.semaphore_wait(barrier, len(partners))

    def pair_of_ids():
        return [ident(), ident()]

    x0, x1r, x1l, x2r, x2l = (pair_of_ids() for _ in range(5))
    d0, d1r, d1l, d2r, d2l = (pair_of_ids() for _ in range(5))
    x3r, x3l, x4r, x4l, d3r, d3l, d4r, d4l = (ident() for _ in range(8))
    s = [ident() for _ in range(10)]
    for h in range(2):
        put(x0[h], x_in.at[h], x_all.at[x, zh, h], z_high)
        put(x1r[h], x_in.at[h], x_all.at[x, zh, h], x_right)
        put(x1l[1 - h], x_in.at[1 - h], x_all.at[x, zh, 1 - h], x_left)
        put(d1r[h], dy_in.at[h], dy_all.at[y, zl, core, h], y_right)
        put(d1l[1 - h], dy_in.at[1 - h], dy_all.at[y, zl, core, 1 - h], y_left)
    for h in range(2):
        put(d0[h], dy_in.at[h], dy_all.at[y, zl, core, h], z_low)
    put(s[0], dy_in, dy_all.at[y, zl, core], sib)

    small[0].wait()
    listed = tiles[...]
    number = lax.broadcasted_iota(jnp.int32, (8, listed.shape[1]), 0) * 26
    for tile in range(26):
        hit = jnp.where(jnp.broadcast_to(listed, number.shape) == number + tile, 1.0, 0.0)
        flag = jnp.sum(hit, axis=1, keepdims=True)
        mask[:, tile * 128:(tile + 1) * 128] = jnp.broadcast_to(flag, (8, 128))
    down_ext[192:, :] = jnp.zeros((64, 1024), BF16)
    up_ext[192:, :] = jnp.zeros((64, 3328), BF16)
    for copy in small[1:]:
        copy.wait()
    w_copy.wait()

    def masking(step, carry):
        at = pl.ds(pl.multiple_of(step * TILE, TILE), TILE)
        for block in range(8):
            rows = slice(block * 128, (block + 1) * 128)
            keep = mask[block:block + 1, at].astype(BF16)
            w[rows, at] = w[rows, at] * jnp.broadcast_to(keep, (128, TILE))
        return carry

    lax.fori_loop(0, 6, masking, 0)

    def span(chunk):
        return slice(chunk[0] * TILE, (chunk[0] + chunk[1]) * TILE)

    def ring_sum(direct, chunks, view, codes_out, codes_in, z_out, z_in, k, plane, order, left, right, opposite, z_device, finish):
        far, lower, upper = lax.rem(k + 2, 4), lax.rem(k + 3, 4), lax.rem(k + 1, 4)
        ids = [[(ident(), ident(), scale_id()) for _ in range(3)] for _ in range(4)]
        z_ids = [(ident(), ident(), scale_id()) for _ in range(2)]

        def where(n):
            return order[n // 2], span(chunks[n % 2])

        def post(key, value, code_out, code_in, device):
            data, scales, slot = key
            encode(value, code_out, scale_out.at[slot])
            put(data, code_out, code_in, device)
            put(scales, scale_out.at[slot], scale_in.at[slot], device)

        def take(key, code_in):
            data, scales, slot = key
            got(data, code_in)
            got(scales, scale_in.at[slot])
            return decode(code_in, scale_in.at[slot])

        def hop(n, i, value, device):
            h, at = where(n)
            post(ids[n][i], value, codes_out.at[i, h, :, at], codes_in.at[i, h, :, at], device)

        def came(n, i):
            h, at = where(n)
            return take(ids[n][i], codes_in.at[i, h, :, at])

        def first(n):
            h, at = where(n)
            hop(n, 0, view(h, far, at)[...], opposite if direct else (left, right)[n % 2])
            if direct or n % 2 == 0:
                hop(n, 2, view(h, upper, at)[...], right)
            if direct or n % 2 == 1:
                hop(n, 1, view(h, lower, at)[...], left)

        def second(n):
            if direct:
                return
            h, at = where(n)
            if n % 2 == 0:
                hop(n, 1, view(h, lower, at)[...] + came(n, 0), left)
            else:
                hop(n, 2, view(h, upper, at)[...] + came(n, 0), right)

        def third(n):
            h, at = where(n)
            total = view(h, k, at)
            value = total[...] + came(n, 1) + came(n, 2)
            total[...] = value + came(n, 0) if direct else value

        def across(j):
            at = span(chunks[j])
            post(z_ids[j], view(1 - plane, k, at)[...], z_out.at[:, at], z_in.at[:, at], z_device)

        def last(j):
            at = span(chunks[j])
            finish[:, at] = (view(plane, k, at)[...] + take(z_ids[j], z_in.at[:, at])).astype(BF16)

        return first, second, third, across, last

    def p_view(h, k, at):
        return p.at[h, k, core, :, at]

    def q_view(h, k, at):
        return q.at[h, k, :, at]

    p_first, p_second, p_third, p_across, p_last = ring_sum(
        P_DIRECT, P_CHUNKS, p_view, p_out, p_in, pz_out, pz_in, y, zl, (zh, zho), y_left, y_right, y_far, z_low, out)
    q_first, q_second, q_third, q_across, q_last = ring_sum(
        Q_DIRECT, G_CHUNKS, q_view, q_out, q_in, qz_out, qz_in, x, zh, (zl, zlo), x_left, x_right, x_far, z_high, gx_out)
    pair_ids = [ident() for _ in range(4)]

    def x_rows(h):
        return x_all[:, h].reshape(256, 1024)

    def p_low(h):
        parts = split_terms(dot_t(x_rows(h), down_ext[:128, :]))
        x_low[h, :, :128] = parts[0]
        x_low[h, :, 128:] = parts[1]

    def p_compute(n):
        h = (zh, zho)[n // 2]

        def step(i, carry):
            at = pl.ds(pl.multiple_of(i * TILE, TILE), TILE)
            value = dot(x_rows(h), w[:, at]) + dot(x_low[h], up_ext[:, at])
            p[h, :, :, :, at] = value.reshape(4, 2, 32, TILE)
            return carry

        begin, count = P_CHUNKS[n % 2]
        lax.fori_loop(begin, begin + count, step, 0, unroll=True)
        at = span(P_CHUNKS[n % 2])
        put(pair_ids[n], p.at[h, :, other, :, at], p_sib.at[h, :, :, at], sib)

    def p_pair(n):
        h, at = (zh, zho)[n // 2], span(P_CHUNKS[n % 2])
        got(pair_ids[n], p_sib.at[h, :, :, at])
        p[h, :, core, :, at] = p[h, :, core, :, at] + p_sib[h, :, :, at]
        p_first(n)

    def dy_rows(h):
        return dy_all[:, h].reshape(256, 3328)

    def q_low(h):
        parts = split_terms(dot_t(dy_rows(h), up_ext[:128, :]))
        dy_low[h, :, :128] = parts[0]
        dy_low[h, :, 128:] = parts[1]

    def q_compute(n):
        h = (zl, zlo)[n // 2]

        def step(i, carry):
            at = pl.ds(pl.multiple_of(i * TILE, TILE), TILE)
            value = dot_t(dy_rows(h), w[at, :]) + dot(dy_low[h], down_ext[:, at])
            q[h, :, :, at] = value.reshape(4, 64, TILE)
            return carry

        begin, count = G_CHUNKS[n % 2]
        lax.fori_loop(begin, begin + count, step, 0, unroll=True)
        q_first(n)

    def gw_compute(begin, end):
        def step(i, carry):
            at = pl.ds(pl.multiple_of(i * TILE, TILE), TILE)
            for half in range(2):
                rows = slice(half * 512, (half + 1) * 512)
                value = dot(x_t[rows, :], dy_all[:, :, :, :, :, at].reshape(512, TILE))
                for block in range(4):
                    keep = mask[half * 4 + block:half * 4 + block + 1, at] * (1.0 / math.sqrt(512))
                    gw[half * 512 + block * 128:half * 512 + (block + 1) * 128, at] = (
                        value[block * 128:(block + 1) * 128] * keep).astype(BF16)
            return carry

        lax.fori_loop(begin, end, step, 0, unroll=True)

    for h in range(2):
        got(x0[h], x_all.at[x, zho, h])
    for h in range(2):
        relay(x2r[h], x_all.at[x, zho, h], x_right)
        relay(x2l[1 - h], x_all.at[x, zho, 1 - h], x_left)
    got(x1r[0], x_all.at[xl, zh, 0])
    relay(x3r, x_all.at[xl, zh, 0], x_right)
    got(x1l[1], x_all.at[xr, zh, 1])
    relay(x3l, x_all.at[xr, zh, 1], x_left)
    got(d1r[0], dy_all.at[yl, zl, core, 0])
    relay(d3r, dy_all.at[yl, zl, core, 0], y_right)
    got(d1l[1], dy_all.at[yr, zl, core, 1])
    relay(d3l, dy_all.at[yr, zl, core, 1], y_left)
    lax.fori_loop(6, 13, masking, 0)
    got(d0[0], dy_all.at[y, zlo, core, 0])
    relay(d2r[0], dy_all.at[y, zlo, core, 0], y_right)
    got(d0[1], dy_all.at[y, zlo, core, 1])
    relay(d2l[1], dy_all.at[y, zlo, core, 1], y_left)
    relay(d2r[1], dy_all.at[y, zlo, core, 1], y_right)
    relay(d2l[0], dy_all.at[y, zlo, core, 0], y_left)
    relay(s[1], dy_all.at[y, zlo, core], sib)
    got(x2r[0], x_all.at[xl, zho, 0])
    relay(x4r, x_all.at[xl, zho, 0], x_right)
    got(x2l[1], x_all.at[xr, zho, 1])
    relay(x4l, x_all.at[xr, zho, 1], x_left)
    got(x1r[1], x_all.at[xl, zh, 1])
    got(x1l[0], x_all.at[xr, zh, 0])
    got(x3r, x_all.at[xo, zh, 0])
    got(x3l, x_all.at[xo, zh, 1])
    x_copy.wait()
    p_low(zh)
    p_compute(0)
    got(d1r[1], dy_all.at[yl, zl, core, 1])
    relay(s[2], dy_all.at[yl, zl, core], sib)
    got(d1l[0], dy_all.at[yr, zl, core, 0])
    relay(s[3], dy_all.at[yr, zl, core], sib)
    got(d2r[0], dy_all.at[yl, zlo, core, 0])
    relay(d4r, dy_all.at[yl, zlo, core, 0], y_right)
    got(d2l[1], dy_all.at[yr, zlo, core, 1])
    relay(d4l, dy_all.at[yr, zlo, core, 1], y_left)
    p_compute(1)
    p_pair(0)
    got(d3r, dy_all.at[yo, zl, core, 0])
    relay(s[6], dy_all.at[yo, zl, core, 0], sib)
    got(d3l, dy_all.at[yo, zl, core, 1])
    relay(s[7], dy_all.at[yo, zl, core, 1], sib)
    got(x2r[1], x_all.at[xl, zho, 1])
    got(x2l[0], x_all.at[xr, zho, 0])
    got(x4r, x_all.at[xo, zho, 0])
    got(x4l, x_all.at[xo, zho, 1])
    p_low(zho)
    p_compute(2)
    p_pair(1)
    p_compute(3)
    p_pair(2)
    got(d2r[1], dy_all.at[yl, zlo, core, 1])
    relay(s[4], dy_all.at[yl, zlo, core], sib)
    got(d2l[0], dy_all.at[yr, zlo, core, 0])
    relay(s[5], dy_all.at[yr, zlo, core], sib)
    p_pair(3)
    dy_copy.wait()
    got(s[0], dy_all.at[y, zl, other])
    got(s[2], dy_all.at[yl, zl, other])
    got(s[3], dy_all.at[yr, zl, other])
    got(s[6], dy_all.at[yo, zl, other, 0])
    got(s[7], dy_all.at[yo, zl, other, 1])
    q_low(zl)
    q_compute(0)
    p_second(0)
    q_compute(1)
    p_second(1)
    got(d4r, dy_all.at[yo, zlo, core, 0])
    relay(s[8], dy_all.at[yo, zlo, core, 0], sib)
    got(d4l, dy_all.at[yo, zlo, core, 1])
    relay(s[9], dy_all.at[yo, zlo, core, 1], sib)
    for quarter in range(4):
        cols = slice(quarter * 256, (quarter + 1) * 256)
        x_t[cols, :] = x_all[:, :, :, :, cols].reshape(512, 256).T
    p_second(2)
    got(s[1], dy_all.at[y, zlo, other])
    got(s[4], dy_all.at[yl, zlo, other])
    got(s[5], dy_all.at[yr, zlo, other])
    got(s[8], dy_all.at[yo, zlo, other, 0])
    got(s[9], dy_all.at[yo, zlo, other, 1])
    q_low(zlo)
    q_compute(2)
    q_second(0)
    p_second(3)
    q_compute(3)
    q_second(1)
    gw_compute(0, 3)
    q_second(2)
    p_third(0)
    gw_compute(3, 5)
    q_second(3)
    p_third(1)
    gw_compute(5, 7)
    q_third(0)
    q_third(1)
    p_third(2)
    p_across(0)
    gw_compute(7, 9)
    q_third(2)
    q_across(0)
    p_third(3)
    p_across(1)
    q_third(3)
    q_across(1)
    gw_compute(9, 13)
    p_last(0)
    q_last(0)
    p_last(1)
    q_last(1)
    for copy in sends:
        copy.wait_send()


def store(out, gx, gw, out_to, gx_to, gw_to, sems):
    pairs = [(gw.at[pl.ds(128 * i, 128)], gw_to.at[pl.ds(128 * i, 128)]) for i in range(8)]
    pairs += [(out, out_to), (gx, gx_to)]
    copies = [pltpu.make_async_copy(src, dst, sems.at[i]) for i, (src, dst) in enumerate(pairs)]
    for copy in copies:
        copy.start()
    for copy in copies:
        copy.wait()


def body(tokens, weight, down, up, grad_out, tile_list):
    anywhere = pl.BlockSpec(memory_space=pl.ANY)
    vmem = pl.BlockSpec(memory_space=pltpu.VMEM)
    scratch = [
        pltpu.VMEM((4, 2, 2, 32, 1024), BF16),
        pltpu.VMEM((4, 2, 2, 2, 16, 3328), BF16),
        pltpu.VMEM((1024, 3328), BF16),
        pltpu.VMEM((1, 156), jnp.int32),
        pltpu.VMEM((8, 3328), F32),
        pltpu.VMEM((256, 3328), BF16),
        pltpu.VMEM((256, 1024), BF16),
        pltpu.VMEM((2, 256, 256), BF16),
        pltpu.VMEM((2, 256, 256), BF16),
        pltpu.VMEM((1024, 512), BF16),
        pltpu.VMEM((2, 4, 2, 32, 3328), F32),
        pltpu.VMEM((2, 4, 32, 3328), F32),
        pltpu.VMEM((3, 2, 32, 3328), I16),
        pltpu.VMEM((3, 2, 32, 3328), I16),
        pltpu.VMEM((32, 3328), I16),
        pltpu.VMEM((32, 3328), I16),
        pltpu.VMEM((2, 4, 64, 1024), F32),
        pltpu.VMEM((3, 2, 64, 1024), I16),
        pltpu.VMEM((3, 2, 64, 1024), I16),
        pltpu.VMEM((64, 1024), I16),
        pltpu.VMEM((64, 1024), I16),
        pltpu.VMEM((28, 8, 128), F32),
        pltpu.VMEM((28, 8, 128), F32),
        pltpu.SemaphoreType.DMA((N_SEM,)),
        pltpu.SemaphoreType.DMA((N_SEM,)),
        pltpu.SemaphoreType.DMA((10,)),
    ]
    shapes = ((32, 3328), (64, 1024), (1024, 3328))
    results = pl.pallas_call(
        kernel,
        out_shape=tuple(pltpu.VMEM(shape, BF16) for shape in shapes),
        in_specs=[pl.BlockSpec(memory_space=pltpu.HBM)] * 6,
        out_specs=(vmem, vmem, vmem),
        scratch_shapes=scratch,
        compiler_params=pltpu.CompilerParams(
            collective_id=0, has_side_effects=True, vmem_limit_bytes=57 * 2**20),
        cost_estimate=pl.CostEstimate(flops=3 * 2 * 512 * 1024 * 3328, bytes_accessed=14 * 2**20, transcendentals=0),
    )(tokens.reshape(2, 32, 1024), weight, down.T, up, grad_out.reshape(2, 16, 3328), tile_list.reshape(1, -1))
    return pl.pallas_call(
        store,
        out_shape=tuple(jax.ShapeDtypeStruct(shape, BF16) for shape in shapes),
        in_specs=[vmem] * 3,
        out_specs=(anywhere,) * 3,
        scratch_shapes=[pltpu.SemaphoreType.DMA((10,))],
        compiler_params=pltpu.CompilerParams(vmem_limit_bytes=2**20),
        cost_estimate=pl.CostEstimate(flops=0, bytes_accessed=8 * 2**20, transcendentals=0),
    )(*results)


def solution(mesh):
    return jax.shard_map(
        body,
        mesh=mesh,
        in_specs=(
            P("col", "row"),
            P("row", "col"),
            P("row", None),
            P(None, "col"),
            P("row", "col"),
            P("row", "col", None),
        ),
        out_specs=(P("row", "col"), P("col", "row"), P("row", "col")),
        check_vma=False,
    )
```

```python
import functools
import math

import jax
import jax.numpy as jnp
from jax import lax
from jax.experimental import pallas as pl
from jax.experimental.pallas import tpu as pltpu
from jax.sharding import PartitionSpec as P

MESH = pl.DeviceIdType.MESH
F32 = jnp.float32
BF16 = jnp.bfloat16
I16 = jnp.int16
TILE = 256
P_CHUNKS = ((0, 7), (7, 6))
G_CHUNKS = ((0, 2), (2, 2))
P_DIRECT, Q_DIRECT = False, True
N_SEM = 128


def dot(a, b):
    return jnp.dot(a, b, preferred_element_type=F32)


def dot_t(a, b):
    return lax.dot_general(a, b, (((1,), (1,)), ((), ())), preferred_element_type=F32)


def split_terms(twice):
    first = lax.broadcasted_iota(jnp.int32, twice.shape, 1) < twice.shape[1] // 2
    high = twice.astype(BF16).astype(F32)
    rest = twice - high
    middle = rest.astype(BF16).astype(F32)
    low = rest - middle
    return (jnp.where(first, high, middle).astype(BF16), jnp.where(first, low, 0.0).astype(BF16))


def diagonal(rows):
    shape = (rows, 128)
    return lax.broadcasted_iota(jnp.int32, shape, 0) == lax.broadcasted_iota(jnp.int32, shape, 1)


def encode(value, code, scale):
    top = jnp.maximum(jnp.max(jnp.abs(value), axis=1, keepdims=True), 1e-30)
    code[...] = jnp.round(value * (32760.0 / top)).astype(jnp.int32).astype(jnp.int16)
    row = jnp.sum(jnp.where(diagonal(code.shape[0]), top * (1.0 / 32760.0), 0.0), axis=0, keepdims=True)
    scale[...] = jnp.broadcast_to(row, (8, 128))


def decode(code, scale):
    rows = code.shape[0]
    row = jnp.broadcast_to(scale[0:1, :], (rows, 128))
    column = jnp.sum(jnp.where(diagonal(rows), row, 0.0), axis=1, keepdims=True)
    return code[...].astype(jnp.int32).astype(F32) * column


def kernel(x_in, w_in, down_in, up_in, dy_in, tiles_in, out, gx_out, gw,
           x_all, dy_all, w, tiles, mask, up_ext, down_ext, x_low, dy_low, x_t,
           p, p_sib, p_out, p_in, pz_out, pz_in, q, q_out, q_in, qz_out, qz_in, scale_out, scale_in, send, recv, local):
    r = lax.axis_index("row")
    c = lax.axis_index("col")
    core = lax.rem(r, 2)
    y, zl = r // 4, lax.rem(r // 2, 2)
    x, zh = c // 2, lax.rem(c, 2)
    other, zlo, zho = 1 - core, 1 - zl, 1 - zh
    yl, yr, yo = lax.rem(y + 3, 4), lax.rem(y + 1, 4), lax.rem(y + 2, 4)
    xl, xr, xo = lax.rem(x + 3, 4), lax.rem(x + 1, 4), lax.rem(x + 2, 4)
    sib, z_low, z_high = (r + 1 - 2 * core, c), (r + 2 - 4 * zl, c), (r, c + 1 - 2 * zh)
    y_left, y_right = (lax.rem(r + 12, 16), c), (lax.rem(r + 4, 16), c)
    x_left, x_right = (r, lax.rem(c + 6, 8)), (r, lax.rem(c + 2, 8))
    y_far, x_far = (lax.rem(r + 8, 16), c), (r, lax.rem(c + 4, 8))

    counter = [0]
    sends = []

    def ident():
        counter[0] += 1
        return counter[0] - 1

    scale_counter = [0]

    def scale_id():
        scale_counter[0] += 1
        return scale_counter[0] - 1

    def put(i, src, dst, device):
        copy = pltpu.make_async_remote_copy(
            src_ref=src, dst_ref=dst, send_sem=send.at[i], recv_sem=recv.at[i],
            device_id=device, device_id_type=MESH)
        copy.start()
        sends.append(copy)

    def relay(i, ref, device):
        put(i, ref, ref, device)

    def got(i, dst):
        pltpu.make_async_remote_copy(
            src_ref=dst, dst_ref=dst, send_sem=send.at[i], recv_sem=recv.at[i],
            device_id=sib, device_id_type=MESH).wait_recv()

    w_copy = pltpu.make_async_copy(w_in, w, local.at[0])
    w_copy.start()
    x_copy = pltpu.make_async_copy(x_in, x_all.at[x, zh], local.at[1])
    x_copy.start()
    dy_copy = pltpu.make_async_copy(dy_in, dy_all.at[y, zl, core], local.at[2])
    dy_copy.start()
    small = [pltpu.make_async_copy(tiles_in, tiles, local.at[3])]
    for part in range(3):
        rows = slice(64 * part, 64 * (part + 1))
        small.append(pltpu.make_async_copy(down_in, down_ext.at[rows], local.at[4 + part]))
        small.append(pltpu.make_async_copy(up_in, up_ext.at[rows], local.at[7 + part]))
    for copy in small:
        copy.start()

    barrier = pltpu.get_barrier_semaphore()
    partners = [sib, y_left, y_right, z_low, x_left, x_right, z_high]
    partners += [y_far] * P_DIRECT + [x_far] * Q_DIRECT
    for device in partners:
        pl.semaphore_signal(barrier, inc=1, device_id=device, device_id_type=MESH)
    pl.semaphore_wait(barrier, len(partners))

    def pair_of_ids():
        return [ident(), ident()]

    x0, x1r, x1l, x2r, x2l = (pair_of_ids() for _ in range(5))
    d0, d1r, d1l, d2r, d2l = (pair_of_ids() for _ in range(5))
    x3r, x3l, x4r, x4l, d3r, d3l, d4r, d4l = (ident() for _ in range(8))
    s = [ident() for _ in range(10)]
    for h in range(2):
        put(x0[h], x_in.at[h], x_all.at[x, zh, h], z_high)
        put(x1r[h], x_in.at[h], x_all.at[x, zh, h], x_right)
        put(x1l[1 - h], x_in.at[1 - h], x_all.at[x, zh, 1 - h], x_left)
        put(d1r[h], dy_in.at[h], dy_all.at[y, zl, core, h], y_right)
        put(d1l[1 - h], dy_in.at[1 - h], dy_all.at[y, zl, core, 1 - h], y_left)
    for h in range(2):
        put(d0[h], dy_in.at[h], dy_all.at[y, zl, core, h], z_low)
    put(s[0], dy_in, dy_all.at[y, zl, core], sib)

    small[0].wait()
    listed = tiles[...]
    number = lax.broadcasted_iota(jnp.int32, (8, listed.shape[1]), 0) * 26
    for tile in range(26):
        hit = jnp.where(jnp.broadcast_to(listed, number.shape) == number + tile, 1.0, 0.0)
        flag = jnp.sum(hit, axis=1, keepdims=True)
        mask[:, tile * 128:(tile + 1) * 128] = jnp.broadcast_to(flag, (8, 128))
    down_ext[192:, :] = jnp.zeros((64, 1024), BF16)
    up_ext[192:, :] = jnp.zeros((64, 3328), BF16)
    for copy in small[1:]:
        copy.wait()
    w_copy.wait()

    def masking(step, carry):
        at = pl.ds(pl.multiple_of(step * TILE, TILE), TILE)
        for block in range(8):
            rows = slice(block * 128, (block + 1) * 128)
            keep = mask[block:block + 1, at].astype(BF16)
            w[rows, at] = w[rows, at] * jnp.broadcast_to(keep, (128, TILE))
        return carry

    lax.fori_loop(0, 6, masking, 0)

    def span(chunk):
        return slice(chunk[0] * TILE, (chunk[0] + chunk[1]) * TILE)

    def ring_sum(direct, chunks, view, codes_out, codes_in, z_out, z_in, k, plane, order, left, right, opposite, z_device, finish):
        far, lower, upper = lax.rem(k + 2, 4), lax.rem(k + 3, 4), lax.rem(k + 1, 4)
        ids = [[(ident(), ident(), scale_id()) for _ in range(3)] for _ in range(4)]
        z_ids = [(ident(), ident(), scale_id()) for _ in range(2)]

        def where(n):
            return order[n // 2], span(chunks[n % 2])

        def post(key, value, code_out, code_in, device):
            data, scales, slot = key
            encode(value, code_out, scale_out.at[slot])
            put(data, code_out, code_in, device)
            put(scales, scale_out.at[slot], scale_in.at[slot], device)

        def take(key, code_in):
            data, scales, slot = key
            got(data, code_in)
            got(scales, scale_in.at[slot])
            return decode(code_in, scale_in.at[slot])

        def hop(n, i, value, device):
            h, at = where(n)
            post(ids[n][i], value, codes_out.at[i, h, :, at], codes_in.at[i, h, :, at], device)

        def came(n, i):
            h, at = where(n)
            return take(ids[n][i], codes_in.at[i, h, :, at])

        def first(n):
            h, at = where(n)
            hop(n, 0, view(h, far, at)[...], opposite if direct else (left, right)[n % 2])
            if direct or n % 2 == 0:
                hop(n, 2, view(h, upper, at)[...], right)
            if direct or n % 2 == 1:
                hop(n, 1, view(h, lower, at)[...], left)

        def second(n):
            if direct:
                return
            h, at = where(n)
            if n % 2 == 0:
                hop(n, 1, view(h, lower, at)[...] + came(n, 0), left)
            else:
                hop(n, 2, view(h, upper, at)[...] + came(n, 0), right)

        def third(n):
            h, at = where(n)
            total = view(h, k, at)
            value = total[...] + came(n, 1) + came(n, 2)
            total[...] = value + came(n, 0) if direct else value

        def across(j):
            at = span(chunks[j])
            post(z_ids[j], view(1 - plane, k, at)[...], z_out.at[:, at], z_in.at[:, at], z_device)

        def last(j):
            at = span(chunks[j])
            finish[:, at] = (view(plane, k, at)[...] + take(z_ids[j], z_in.at[:, at])).astype(BF16)

        return first, second, third, across, last

    def p_view(h, k, at):
        return p.at[h, k, core, :, at]

    def q_view(h, k, at):
        return q.at[h, k, :, at]

    p_first, p_second, p_third, p_across, p_last = ring_sum(
        P_DIRECT, P_CHUNKS, p_view, p_out, p_in, pz_out, pz_in, y, zl, (zh, zho), y_left, y_right, y_far, z_low, out)
    q_first, q_second, q_third, q_across, q_last = ring_sum(
        Q_DIRECT, G_CHUNKS, q_view, q_out, q_in, qz_out, qz_in, x, zh, (zl, zlo), x_left, x_right, x_far, z_high, gx_out)
    pair_ids = [ident() for _ in range(4)]

    def x_rows(h):
        return x_all[:, h].reshape(256, 1024)

    def p_low(h):
        parts = split_terms(dot_t(x_rows(h), down_ext[:128, :]))
        x_low[h, :, :128] = parts[0]
        x_low[h, :, 128:] = parts[1]

    def p_compute(n):
        h = (zh, zho)[n // 2]

        def step(i, carry):
            at = pl.ds(pl.multiple_of(i * TILE, TILE), TILE)
            value = dot(x_rows(h), w[:, at]) + dot(x_low[h], up_ext[:, at])
            p[h, :, :, :, at] = value.reshape(4, 2, 32, TILE)
            return carry

        begin, count = P_CHUNKS[n % 2]
        lax.fori_loop(begin, begin + count, step, 0, unroll=True)
        at = span(P_CHUNKS[n % 2])
        put(pair_ids[n], p.at[h, :, other, :, at], p_sib.at[h, :, :, at], sib)

    def p_pair(n):
        h, at = (zh, zho)[n // 2], span(P_CHUNKS[n % 2])
        got(pair_ids[n], p_sib.at[h, :, :, at])
        p[h, :, core, :, at] = p[h, :, core, :, at] + p_sib[h, :, :, at]
        p_first(n)

    def dy_rows(h):
        return dy_all[:, h].reshape(256, 3328)

    def q_low(h):
        parts = split_terms(dot_t(dy_rows(h), up_ext[:128, :]))
        dy_low[h, :, :128] = parts[0]
        dy_low[h, :, 128:] = parts[1]

    def q_compute(n):
        h = (zl, zlo)[n // 2]

        def step(i, carry):
            at = pl.ds(pl.multiple_of(i * TILE, TILE), TILE)
            value = dot_t(dy_rows(h), w[at, :]) + dot(dy_low[h], down_ext[:, at])
            q[h, :, :, at] = value.reshape(4, 64, TILE)
            return carry

        begin, count = G_CHUNKS[n % 2]
        lax.fori_loop(begin, begin + count, step, 0, unroll=True)
        q_first(n)

    def gw_compute(begin, end):
        def step(i, carry):
            at = pl.ds(pl.multiple_of(i * TILE, TILE), TILE)
            for half in range(2):
                rows = slice(half * 512, (half + 1) * 512)
                value = dot(x_t[rows, :], dy_all[:, :, :, :, :, at].reshape(512, TILE))
                for block in range(4):
                    keep = mask[half * 4 + block:half * 4 + block + 1, at] * (1.0 / math.sqrt(512))
                    gw[half * 512 + block * 128:half * 512 + (block + 1) * 128, at] = (
                        value[block * 128:(block + 1) * 128] * keep).astype(BF16)
            return carry

        lax.fori_loop(begin, end, step, 0, unroll=True)

    for h in range(2):
        got(x0[h], x_all.at[x, zho, h])
    for h in range(2):
        relay(x2r[h], x_all.at[x, zho, h], x_right)
        relay(x2l[1 - h], x_all.at[x, zho, 1 - h], x_left)
    got(x1r[0], x_all.at[xl, zh, 0])
    relay(x3r, x_all.at[xl, zh, 0], x_right)
    got(x1l[1], x_all.at[xr, zh, 1])
    relay(x3l, x_all.at[xr, zh, 1], x_left)
    got(d1r[0], dy_all.at[yl, zl, core, 0])
    relay(d3r, dy_all.at[yl, zl, core, 0], y_right)
    got(d1l[1], dy_all.at[yr, zl, core, 1])
    relay(d3l, dy_all.at[yr, zl, core, 1], y_left)
    lax.fori_loop(6, 13, masking, 0)
    got(x1r[1], x_all.at[xl, zh, 1])
    got(x1l[0], x_all.at[xr, zh, 0])
    got(x3r, x_all.at[xo, zh, 0])
    got(x3l, x_all.at[xo, zh, 1])
    x_copy.wait()
    p_low(zh)
    p_compute(0)
    got(x2r[0], x_all.at[xl, zho, 0])
    relay(x4r, x_all.at[xl, zho, 0], x_right)
    got(x2l[1], x_all.at[xr, zho, 1])
    relay(x4l, x_all.at[xr, zho, 1], x_left)
    got(d0[0], dy_all.at[y, zlo, core, 0])
    relay(d2r[0], dy_all.at[y, zlo, core, 0], y_right)
    got(d0[1], dy_all.at[y, zlo, core, 1])
    relay(d2l[1], dy_all.at[y, zlo, core, 1], y_left)
    relay(d2r[1], dy_all.at[y, zlo, core, 1], y_right)
    relay(d2l[0], dy_all.at[y, zlo, core, 0], y_left)
    relay(s[1], dy_all.at[y, zlo, core], sib)
    got(d1r[1], dy_all.at[yl, zl, core, 1])
    relay(s[2], dy_all.at[yl, zl, core], sib)
    got(d1l[0], dy_all.at[yr, zl, core, 0])
    relay(s[3], dy_all.at[yr, zl, core], sib)
    got(d3r, dy_all.at[yo, zl, core, 0])
    relay(d4r, dy_all.at[yo, zl, core, 0], z_low)
    got(d3l, dy_all.at[yo, zl, core, 1])
    relay(d4l, dy_all.at[yo, zl, core, 1], z_low)
    relay(s[6], dy_all.at[yo, zl, core, 0], sib)
    relay(s[7], dy_all.at[yo, zl, core, 1], sib)
    p_compute(1)
    p_pair(0)
    got(x2r[1], x_all.at[xl, zho, 1])
    got(x2l[0], x_all.at[xr, zho, 0])
    got(x4r, x_all.at[xo, zho, 0])
    got(x4l, x_all.at[xo, zho, 1])
    p_low(zho)
    p_compute(2)
    p_pair(1)
    p_compute(3)
    p_pair(2)
    got(d2r[0], dy_all.at[yl, zlo, core, 0])
    got(d2r[1], dy_all.at[yl, zlo, core, 1])
    relay(s[4], dy_all.at[yl, zlo, core], sib)
    got(d2l[1], dy_all.at[yr, zlo, core, 1])
    got(d2l[0], dy_all.at[yr, zlo, core, 0])
    relay(s[5], dy_all.at[yr, zlo, core], sib)
    p_pair(3)
    dy_copy.wait()
    got(s[0], dy_all.at[y, zl, other])
    got(s[2], dy_all.at[yl, zl, other])
    got(s[3], dy_all.at[yr, zl, other])
    got(s[6], dy_all.at[yo, zl, other, 0])
    got(s[7], dy_all.at[yo, zl, other, 1])
    q_low(zl)
    q_compute(0)
    p_second(0)
    q_compute(1)
    p_second(1)
    got(d4r, dy_all.at[yo, zlo, core, 0])
    relay(s[8], dy_all.at[yo, zlo, core, 0], sib)
    got(d4l, dy_all.at[yo, zlo, core, 1])
    relay(s[9], dy_all.at[yo, zlo, core, 1], sib)
    for quarter in range(4):
        cols = slice(quarter * 256, (quarter + 1) * 256)
        x_t[cols, :] = x_all[:, :, :, :, cols].reshape(512, 256).T
    p_second(2)
    got(s[1], dy_all.at[y, zlo, other])
    got(s[4], dy_all.at[yl, zlo, other])
    got(s[5], dy_all.at[yr, zlo, other])
    got(s[8], dy_all.at[yo, zlo, other, 0])
    got(s[9], dy_all.at[yo, zlo, other, 1])
    q_low(zlo)
    q_compute(2)
    q_second(0)
    p_second(3)
    q_compute(3)
    q_second(1)
    gw_compute(0, 2)
    p_third(0)
    p_third(1)
    gw_compute(2, 4)
    p_third(2)
    p_across(0)
    q_third(0)
    q_third(1)
    gw_compute(4, 5)
    p_third(3)
    p_across(1)
    gw_compute(5, 6)
    q_third(2)
    q_across(0)
    q_third(3)
    q_across(1)
    gw_compute(6, 13)
    p_last(0)
    p_last(1)
    q_last(0)
    q_last(1)
    for copy in sends:
        copy.wait_send()


def store(out, gx, gw, out_to, gx_to, gw_to, sems):
    pairs = [(gw.at[pl.ds(128 * i, 128)], gw_to.at[pl.ds(128 * i, 128)]) for i in range(8)]
    pairs += [(out, out_to), (gx, gx_to)]
    copies = [pltpu.make_async_copy(src, dst, sems.at[i]) for i, (src, dst) in enumerate(pairs)]
    for copy in copies:
        copy.start()
    for copy in copies:
        copy.wait()


def body(tokens, weight, down, up, grad_out, tile_list):
    anywhere = pl.BlockSpec(memory_space=pl.ANY)
    vmem = pl.BlockSpec(memory_space=pltpu.VMEM)
    scratch = [
        pltpu.VMEM((4, 2, 2, 32, 1024), BF16),
        pltpu.VMEM((4, 2, 2, 2, 16, 3328), BF16),
        pltpu.VMEM((1024, 3328), BF16),
        pltpu.VMEM((1, 156), jnp.int32),
        pltpu.VMEM((8, 3328), F32),
        pltpu.VMEM((256, 3328), BF16),
        pltpu.VMEM((256, 1024), BF16),
        pltpu.VMEM((2, 256, 256), BF16),
        pltpu.VMEM((2, 256, 256), BF16),
        pltpu.VMEM((1024, 512), BF16),
        pltpu.VMEM((2, 4, 2, 32, 3328), F32),
        pltpu.VMEM((2, 4, 32, 3328), F32),
        pltpu.VMEM((3, 2, 32, 3328), I16),
        pltpu.VMEM((3, 2, 32, 3328), I16),
        pltpu.VMEM((32, 3328), I16),
        pltpu.VMEM((32, 3328), I16),
        pltpu.VMEM((2, 4, 64, 1024), F32),
        pltpu.VMEM((3, 2, 64, 1024), I16),
        pltpu.VMEM((3, 2, 64, 1024), I16),
        pltpu.VMEM((64, 1024), I16),
        pltpu.VMEM((64, 1024), I16),
        pltpu.VMEM((28, 8, 128), F32),
        pltpu.VMEM((28, 8, 128), F32),
        pltpu.SemaphoreType.DMA((N_SEM,)),
        pltpu.SemaphoreType.DMA((N_SEM,)),
        pltpu.SemaphoreType.DMA((10,)),
    ]
    shapes = ((32, 3328), (64, 1024), (1024, 3328))
    results = pl.pallas_call(
        kernel,
        out_shape=tuple(pltpu.VMEM(shape, BF16) for shape in shapes),
        in_specs=[pl.BlockSpec(memory_space=pltpu.HBM)] * 6,
        out_specs=(vmem, vmem, vmem),
        scratch_shapes=scratch,
        compiler_params=pltpu.CompilerParams(
            collective_id=0, has_side_effects=True, vmem_limit_bytes=57 * 2**20),
        cost_estimate=pl.CostEstimate(flops=3 * 2 * 512 * 1024 * 3328, bytes_accessed=14 * 2**20, transcendentals=0),
    )(tokens.reshape(2, 32, 1024), weight, down.T, up, grad_out.reshape(2, 16, 3328), tile_list.reshape(1, -1))
    return pl.pallas_call(
        store,
        out_shape=tuple(jax.ShapeDtypeStruct(shape, BF16) for shape in shapes),
        in_specs=[vmem] * 3,
        out_specs=(anywhere,) * 3,
        scratch_shapes=[pltpu.SemaphoreType.DMA((10,))],
        compiler_params=pltpu.CompilerParams(vmem_limit_bytes=2**20),
        cost_estimate=pl.CostEstimate(flops=0, bytes_accessed=8 * 2**20, transcendentals=0),
    )(*results)


def solution(mesh):
    return jax.shard_map(
        body,
        mesh=mesh,
        in_specs=(
            P("col", "row"),
            P("row", "col"),
            P("row", None),
            P(None, "col"),
            P("row", "col"),
            P("row", "col", None),
        ),
        out_specs=(P("row", "col"), P("col", "row"), P("row", "col")),
        check_vma=False,
    )
```

```python
import functools
import math

import jax
import jax.numpy as jnp
from jax import lax
from jax.experimental import pallas as pl
from jax.experimental.pallas import tpu as pltpu
from jax.sharding import PartitionSpec as P

MESH = pl.DeviceIdType.MESH
F32 = jnp.float32
BF16 = jnp.bfloat16
I16 = jnp.int16
TILE = 256
P_CHUNKS = ((0, 7), (7, 6))
G_CHUNKS = ((0, 2), (2, 2))
P_DIRECT, Q_DIRECT = False, True
N_SEM = 128


def dot(a, b):
    return jnp.dot(a, b, preferred_element_type=F32)


def dot_t(a, b):
    return lax.dot_general(a, b, (((1,), (1,)), ((), ())), preferred_element_type=F32)


def split_terms(twice):
    first = lax.broadcasted_iota(jnp.int32, twice.shape, 1) < twice.shape[1] // 2
    high = twice.astype(BF16).astype(F32)
    rest = twice - high
    middle = rest.astype(BF16).astype(F32)
    low = rest - middle
    return (jnp.where(first, high, middle).astype(BF16), jnp.where(first, low, 0.0).astype(BF16))


def diagonal(rows):
    shape = (rows, 128)
    return lax.broadcasted_iota(jnp.int32, shape, 0) == lax.broadcasted_iota(jnp.int32, shape, 1)


def encode(value, code, scale):
    top = jnp.maximum(jnp.max(jnp.abs(value), axis=1, keepdims=True), 1e-30)
    code[...] = jnp.round(value * (32760.0 / top)).astype(jnp.int32).astype(jnp.int16)
    row = jnp.sum(jnp.where(diagonal(code.shape[0]), top * (1.0 / 32760.0), 0.0), axis=0, keepdims=True)
    scale[...] = jnp.broadcast_to(row, (8, 128))


def decode(code, scale):
    rows = code.shape[0]
    row = jnp.broadcast_to(scale[0:1, :], (rows, 128))
    column = jnp.sum(jnp.where(diagonal(rows), row, 0.0), axis=1, keepdims=True)
    return code[...].astype(jnp.int32).astype(F32) * column


def kernel(x_in, w_in, down_in, up_in, dy_in, tiles_in, out, gx_out, gw,
           x_all, dy_all, w, tiles, mask, up_ext, down_ext, x_low, dy_low, x_t,
           p, p_sib, p_out, p_in, pz_out, pz_in, q, q_out, q_in, qz_out, qz_in, scale_out, scale_in, send, recv, local):
    r = lax.axis_index("row")
    c = lax.axis_index("col")
    core = lax.rem(r, 2)
    y, zl = r // 4, lax.rem(r // 2, 2)
    x, zh = c // 2, lax.rem(c, 2)
    other, zlo, zho = 1 - core, 1 - zl, 1 - zh
    yl, yr, yo = lax.rem(y + 3, 4), lax.rem(y + 1, 4), lax.rem(y + 2, 4)
    xl, xr, xo = lax.rem(x + 3, 4), lax.rem(x + 1, 4), lax.rem(x + 2, 4)
    sib, z_low, z_high = (r + 1 - 2 * core, c), (r + 2 - 4 * zl, c), (r, c + 1 - 2 * zh)
    y_left, y_right = (lax.rem(r + 12, 16), c), (lax.rem(r + 4, 16), c)
    x_left, x_right = (r, lax.rem(c + 6, 8)), (r, lax.rem(c + 2, 8))
    y_far, x_far = (lax.rem(r + 8, 16), c), (r, lax.rem(c + 4, 8))

    counter = [0]
    sends = []

    def ident():
        counter[0] += 1
        return counter[0] - 1

    scale_counter = [0]

    def scale_id():
        scale_counter[0] += 1
        return scale_counter[0] - 1

    def put(i, src, dst, device):
        copy = pltpu.make_async_remote_copy(
            src_ref=src, dst_ref=dst, send_sem=send.at[i], recv_sem=recv.at[i],
            device_id=device, device_id_type=MESH)
        copy.start()
        sends.append(copy)

    def relay(i, ref, device):
        put(i, ref, ref, device)

    def got(i, dst):
        pltpu.make_async_remote_copy(
            src_ref=dst, dst_ref=dst, send_sem=send.at[i], recv_sem=recv.at[i],
            device_id=sib, device_id_type=MESH).wait_recv()

    w_copy = pltpu.make_async_copy(w_in, w, local.at[0])
    w_copy.start()
    x_copy = pltpu.make_async_copy(x_in, x_all.at[x, zh], local.at[1])
    x_copy.start()
    dy_copy = pltpu.make_async_copy(dy_in, dy_all.at[y, zl, core], local.at[2])
    dy_copy.start()
    small = [pltpu.make_async_copy(tiles_in, tiles, local.at[3])]
    for part in range(3):
        rows = slice(64 * part, 64 * (part + 1))
        small.append(pltpu.make_async_copy(down_in, down_ext.at[rows], local.at[4 + part]))
        small.append(pltpu.make_async_copy(up_in, up_ext.at[rows], local.at[7 + part]))
    for copy in small:
        copy.start()

    barrier = pltpu.get_barrier_semaphore()
    partners = [sib, y_left, y_right, z_low, x_left, x_right, z_high]
    partners += [y_far] * P_DIRECT + [x_far] * Q_DIRECT
    for device in partners:
        pl.semaphore_signal(barrier, inc=1, device_id=device, device_id_type=MESH)
    pl.semaphore_wait(barrier, len(partners))

    def pair_of_ids():
        return [ident(), ident()]

    x0, x1r, x1l, x2r, x2l = (pair_of_ids() for _ in range(5))
    d0, d1r, d1l, d2r, d2l = (pair_of_ids() for _ in range(5))
    x3r, x3l, x4r, x4l, d3r, d3l, d4r, d4l = (ident() for _ in range(8))
    s = [ident() for _ in range(10)]
    for h in range(2):
        put(x0[h], x_in.at[h], x_all.at[x, zh, h], z_high)
        put(x1r[h], x_in.at[h], x_all.at[x, zh, h], x_right)
        put(x1l[1 - h], x_in.at[1 - h], x_all.at[x, zh, 1 - h], x_left)
        put(d1r[h], dy_in.at[h], dy_all.at[y, zl, core, h], y_right)
        put(d1l[1 - h], dy_in.at[1 - h], dy_all.at[y, zl, core, 1 - h], y_left)
    for h in range(2):
        put(d0[h], dy_in.at[h], dy_all.at[y, zl, core, h], z_low)
    put(s[0], dy_in, dy_all.at[y, zl, core], sib)

    small[0].wait()
    listed = tiles[...]
    number = lax.broadcasted_iota(jnp.int32, (8, listed.shape[1]), 0) * 26
    for tile in range(26):
        hit = jnp.where(jnp.broadcast_to(listed, number.shape) == number + tile, 1.0, 0.0)
        flag = jnp.sum(hit, axis=1, keepdims=True)
        mask[:, tile * 128:(tile + 1) * 128] = jnp.broadcast_to(flag, (8, 128))
    down_ext[192:, :] = jnp.zeros((64, 1024), BF16)
    up_ext[192:, :] = jnp.zeros((64, 3328), BF16)
    for copy in small[1:]:
        copy.wait()
    w_copy.wait()

    def masking(step, carry):
        at = pl.ds(pl.multiple_of(step * TILE, TILE), TILE)
        for block in range(8):
            rows = slice(block * 128, (block + 1) * 128)
            keep = mask[block:block + 1, at].astype(BF16)
            w[rows, at] = w[rows, at] * jnp.broadcast_to(keep, (128, TILE))
        return carry

    lax.fori_loop(0, 6, masking, 0)

    def span(chunk):
        return slice(chunk[0] * TILE, (chunk[0] + chunk[1]) * TILE)

    def ring_sum(direct, chunks, view, codes_out, codes_in, z_out, z_in, k, plane, order, left, right, opposite, z_device, finish):
        far, lower, upper = lax.rem(k + 2, 4), lax.rem(k + 3, 4), lax.rem(k + 1, 4)
        ids = [[(ident(), ident(), scale_id()) for _ in range(3)] for _ in range(4)]
        z_ids = [(ident(), ident(), scale_id()) for _ in range(2)]

        def where(n):
            return order[n // 2], span(chunks[n % 2])

        def post(key, value, code_out, code_in, device):
            data, scales, slot = key
            encode(value, code_out, scale_out.at[slot])
            put(data, code_out, code_in, device)
            put(scales, scale_out.at[slot], scale_in.at[slot], device)

        def take(key, code_in):
            data, scales, slot = key
            got(data, code_in)
            got(scales, scale_in.at[slot])
            return decode(code_in, scale_in.at[slot])

        def hop(n, i, value, device):
            h, at = where(n)
            post(ids[n][i], value, codes_out.at[i, h, :, at], codes_in.at[i, h, :, at], device)

        def came(n, i):
            h, at = where(n)
            return take(ids[n][i], codes_in.at[i, h, :, at])

        def first(n):
            h, at = where(n)
            hop(n, 0, view(h, far, at)[...], opposite if direct else (left, right)[n % 2])
            if direct or n % 2 == 0:
                hop(n, 2, view(h, upper, at)[...], right)
            if direct or n % 2 == 1:
                hop(n, 1, view(h, lower, at)[...], left)

        def second(n):
            if direct:
                return
            h, at = where(n)
            if n % 2 == 0:
                hop(n, 1, view(h, lower, at)[...] + came(n, 0), left)
            else:
                hop(n, 2, view(h, upper, at)[...] + came(n, 0), right)

        def third(n):
            h, at = where(n)
            total = view(h, k, at)
            value = total[...] + came(n, 1) + came(n, 2)
            total[...] = value + came(n, 0) if direct else value

        def across(j):
            at = span(chunks[j])
            post(z_ids[j], view(1 - plane, k, at)[...], z_out.at[:, at], z_in.at[:, at], z_device)

        def last(j):
            at = span(chunks[j])
            finish[:, at] = (view(plane, k, at)[...] + take(z_ids[j], z_in.at[:, at])).astype(BF16)

        return first, second, third, across, last

    def p_view(h, k, at):
        return p.at[h, k, core, :, at]

    def q_view(h, k, at):
        return q.at[h, k, :, at]

    p_first, p_second, p_third, p_across, p_last = ring_sum(
        P_DIRECT, P_CHUNKS, p_view, p_out, p_in, pz_out, pz_in, y, zl, (zh, zho), y_left, y_right, y_far, z_low, out)
    q_first, q_second, q_third, q_across, q_last = ring_sum(
        Q_DIRECT, G_CHUNKS, q_view, q_out, q_in, qz_out, qz_in, x, zh, (zl, zlo), x_left, x_right, x_far, z_high, gx_out)
    pair_ids = [ident() for _ in range(4)]

    def x_rows(h):
        return x_all[:, h].reshape(256, 1024)

    def p_low(h):
        parts = split_terms(dot_t(x_rows(h), down_ext[:128, :]))
        x_low[h, :, :128] = parts[0]
        x_low[h, :, 128:] = parts[1]

    def p_compute(n):
        h = (zh, zho)[n // 2]

        def step(i, carry):
            at = pl.ds(pl.multiple_of(i * TILE, TILE), TILE)
            value = dot(x_rows(h), w[:, at]) + dot(x_low[h], up_ext[:, at])
            p[h, :, :, :, at] = value.reshape(4, 2, 32, TILE)
            return carry

        begin, count = P_CHUNKS[n % 2]
        lax.fori_loop(begin, begin + count, step, 0, unroll=True)
        at = span(P_CHUNKS[n % 2])
        put(pair_ids[n], p.at[h, :, other, :, at], p_sib.at[h, :, :, at], sib)

    def p_pair(n):
        h, at = (zh, zho)[n // 2], span(P_CHUNKS[n % 2])
        got(pair_ids[n], p_sib.at[h, :, :, at])
        p[h, :, core, :, at] = p[h, :, core, :, at] + p_sib[h, :, :, at]
        p_first(n)

    def dy_rows(h):
        return dy_all[:, h].reshape(256, 3328)

    def q_low(h):
        parts = split_terms(dot_t(dy_rows(h), up_ext[:128, :]))
        dy_low[h, :, :128] = parts[0]
        dy_low[h, :, 128:] = parts[1]

    def q_compute(n):
        h = (zl, zlo)[n // 2]

        def step(i, carry):
            at = pl.ds(pl.multiple_of(i * TILE, TILE), TILE)
            value = dot_t(dy_rows(h), w[at, :]) + dot(dy_low[h], down_ext[:, at])
            q[h, :, :, at] = value.reshape(4, 64, TILE)
            return carry

        begin, count = G_CHUNKS[n % 2]
        lax.fori_loop(begin, begin + count, step, 0, unroll=True)
        q_first(n)

    def gw_compute(begin, end):
        def step(i, carry):
            at = pl.ds(pl.multiple_of(i * TILE, TILE), TILE)
            for half in range(2):
                rows = slice(half * 512, (half + 1) * 512)
                value = dot(x_t[rows, :], dy_all[:, :, :, :, :, at].reshape(512, TILE))
                for block in range(4):
                    keep = mask[half * 4 + block:half * 4 + block + 1, at] * (1.0 / math.sqrt(512))
                    gw[half * 512 + block * 128:half * 512 + (block + 1) * 128, at] = (
                        value[block * 128:(block + 1) * 128] * keep).astype(BF16)
            return carry

        lax.fori_loop(begin, end, step, 0, unroll=True)

    for h in range(2):
        got(x0[h], x_all.at[x, zho, h])
    for h in range(2):
        relay(x2r[h], x_all.at[x, zho, h], x_right)
        relay(x2l[1 - h], x_all.at[x, zho, 1 - h], x_left)
    got(x1r[0], x_all.at[xl, zh, 0])
    relay(x3r, x_all.at[xl, zh, 0], x_right)
    got(x1l[1], x_all.at[xr, zh, 1])
    relay(x3l, x_all.at[xr, zh, 1], x_left)
    got(d1r[0], dy_all.at[yl, zl, core, 0])
    relay(d3r, dy_all.at[yl, zl, core, 0], y_right)
    got(d1l[1], dy_all.at[yr, zl, core, 1])
    relay(d3l, dy_all.at[yr, zl, core, 1], y_left)
    lax.fori_loop(6, 13, masking, 0)
    got(x1r[1], x_all.at[xl, zh, 1])
    got(x1l[0], x_all.at[xr, zh, 0])
    got(x3r, x_all.at[xo, zh, 0])
    got(x3l, x_all.at[xo, zh, 1])
    x_copy.wait()
    p_low(zh)
    p_compute(0)
    got(x2r[0], x_all.at[xl, zho, 0])
    relay(x4r, x_all.at[xl, zho, 0], x_right)
    got(x2l[1], x_all.at[xr, zho, 1])
    relay(x4l, x_all.at[xr, zho, 1], x_left)
    got(d0[0], dy_all.at[y, zlo, core, 0])
    relay(d2r[0], dy_all.at[y, zlo, core, 0], y_right)
    got(d0[1], dy_all.at[y, zlo, core, 1])
    relay(d2l[1], dy_all.at[y, zlo, core, 1], y_left)
    relay(s[1], dy_all.at[y, zlo, core], sib)
    got(d1r[1], dy_all.at[yl, zl, core, 1])
    relay(d2r[1], dy_all.at[yl, zl, core, 1], z_low)
    relay(s[2], dy_all.at[yl, zl, core], sib)
    got(d1l[0], dy_all.at[yr, zl, core, 0])
    relay(d2l[0], dy_all.at[yr, zl, core, 0], z_low)
    relay(s[3], dy_all.at[yr, zl, core], sib)
    got(d3r, dy_all.at[yo, zl, core, 0])
    relay(d4r, dy_all.at[yo, zl, core, 0], z_low)
    got(d3l, dy_all.at[yo, zl, core, 1])
    relay(d4l, dy_all.at[yo, zl, core, 1], z_low)
    relay(s[6], dy_all.at[yo, zl, core, 0], sib)
    relay(s[7], dy_all.at[yo, zl, core, 1], sib)
    p_compute(1)
    p_pair(0)
    got(x2r[1], x_all.at[xl, zho, 1])
    got(x2l[0], x_all.at[xr, zho, 0])
    got(x4r, x_all.at[xo, zho, 0])
    got(x4l, x_all.at[xo, zho, 1])
    p_low(zho)
    p_compute(2)
    p_pair(1)
    p_compute(3)
    p_pair(2)
    got(d2r[0], dy_all.at[yl, zlo, core, 0])
    got(d2r[1], dy_all.at[yl, zlo, core, 1])
    relay(s[4], dy_all.at[yl, zlo, core], sib)
    got(d2l[1], dy_all.at[yr, zlo, core, 1])
    got(d2l[0], dy_all.at[yr, zlo, core, 0])
    relay(s[5], dy_all.at[yr, zlo, core], sib)
    p_pair(3)
    dy_copy.wait()
    got(s[0], dy_all.at[y, zl, other])
    got(s[2], dy_all.at[yl, zl, other])
    got(s[3], dy_all.at[yr, zl, other])
    got(s[6], dy_all.at[yo, zl, other, 0])
    got(s[7], dy_all.at[yo, zl, other, 1])
    q_low(zl)
    q_compute(0)
    p_second(0)
    q_compute(1)
    p_second(1)
    got(d4r, dy_all.at[yo, zlo, core, 0])
    relay(s[8], dy_all.at[yo, zlo, core, 0], sib)
    got(d4l, dy_all.at[yo, zlo, core, 1])
    relay(s[9], dy_all.at[yo, zlo, core, 1], sib)
    for quarter in range(4):
        cols = slice(quarter * 256, (quarter + 1) * 256)
        x_t[cols, :] = x_all[:, :, :, :, cols].reshape(512, 256).T
    p_second(2)
    got(s[1], dy_all.at[y, zlo, other])
    got(s[4], dy_all.at[yl, zlo, other])
    got(s[5], dy_all.at[yr, zlo, other])
    got(s[8], dy_all.at[yo, zlo, other, 0])
    got(s[9], dy_all.at[yo, zlo, other, 1])
    q_low(zlo)
    q_compute(2)
    q_second(0)
    p_second(3)
    q_compute(3)
    q_second(1)
    p_third(0)
    gw_compute(0, 2)
    p_third(1)
    q_third(0)
    p_third(2)
    p_across(0)
    gw_compute(2, 4)
    q_third(1)
    q_third(2)
    q_across(0)
    p_third(3)
    p_across(1)
    q_third(3)
    q_across(1)
    gw_compute(4, 13)
    p_last(0)
    q_last(0)
    p_last(1)
    q_last(1)
    for copy in sends:
        copy.wait_send()


def store(out, gx, gw, out_to, gx_to, gw_to, sems):
    pairs = [(gw.at[pl.ds(128 * i, 128)], gw_to.at[pl.ds(128 * i, 128)]) for i in range(8)]
    pairs += [(out, out_to), (gx, gx_to)]
    copies = [pltpu.make_async_copy(src, dst, sems.at[i]) for i, (src, dst) in enumerate(pairs)]
    for copy in copies:
        copy.start()
    for copy in copies:
        copy.wait()


def body(tokens, weight, down, up, grad_out, tile_list):
    anywhere = pl.BlockSpec(memory_space=pl.ANY)
    vmem = pl.BlockSpec(memory_space=pltpu.VMEM)
    scratch = [
        pltpu.VMEM((4, 2, 2, 32, 1024), BF16),
        pltpu.VMEM((4, 2, 2, 2, 16, 3328), BF16),
        pltpu.VMEM((1024, 3328), BF16),
        pltpu.VMEM((1, 156), jnp.int32),
        pltpu.VMEM((8, 3328), F32),
        pltpu.VMEM((256, 3328), BF16),
        pltpu.VMEM((256, 1024), BF16),
        pltpu.VMEM((2, 256, 256), BF16),
        pltpu.VMEM((2, 256, 256), BF16),
        pltpu.VMEM((1024, 512), BF16),
        pltpu.VMEM((2, 4, 2, 32, 3328), F32),
        pltpu.VMEM((2, 4, 32, 3328), F32),
        pltpu.VMEM((3, 2, 32, 3328), I16),
        pltpu.VMEM((3, 2, 32, 3328), I16),
        pltpu.VMEM((32, 3328), I16),
        pltpu.VMEM((32, 3328), I16),
        pltpu.VMEM((2, 4, 64, 1024), F32),
        pltpu.VMEM((3, 2, 64, 1024), I16),
        pltpu.VMEM((3, 2, 64, 1024), I16),
        pltpu.VMEM((64, 1024), I16),
        pltpu.VMEM((64, 1024), I16),
        pltpu.VMEM((28, 8, 128), F32),
        pltpu.VMEM((28, 8, 128), F32),
        pltpu.SemaphoreType.DMA((N_SEM,)),
        pltpu.SemaphoreType.DMA((N_SEM,)),
        pltpu.SemaphoreType.DMA((10,)),
    ]
    shapes = ((32, 3328), (64, 1024), (1024, 3328))
    results = pl.pallas_call(
        kernel,
        out_shape=tuple(pltpu.VMEM(shape, BF16) for shape in shapes),
        in_specs=[pl.BlockSpec(memory_space=pltpu.HBM)] * 6,
        out_specs=(vmem, vmem, vmem),
        scratch_shapes=scratch,
        compiler_params=pltpu.CompilerParams(
            collective_id=0, has_side_effects=True, vmem_limit_bytes=57 * 2**20),
        cost_estimate=pl.CostEstimate(flops=3 * 2 * 512 * 1024 * 3328, bytes_accessed=14 * 2**20, transcendentals=0),
    )(tokens.reshape(2, 32, 1024), weight, down.T, up, grad_out.reshape(2, 16, 3328), tile_list.reshape(1, -1))
    return pl.pallas_call(
        store,
        out_shape=tuple(jax.ShapeDtypeStruct(shape, BF16) for shape in shapes),
        in_specs=[vmem] * 3,
        out_specs=(anywhere,) * 3,
        scratch_shapes=[pltpu.SemaphoreType.DMA((10,))],
        compiler_params=pltpu.CompilerParams(vmem_limit_bytes=2**20),
        cost_estimate=pl.CostEstimate(flops=0, bytes_accessed=8 * 2**20, transcendentals=0),
    )(*results)


def solution(mesh):
    return jax.shard_map(
        body,
        mesh=mesh,
        in_specs=(
            P("col", "row"),
            P("row", "col"),
            P("row", None),
            P(None, "col"),
            P("row", "col"),
            P("row", "col", None),
        ),
        out_specs=(P("row", "col"), P("col", "row"), P("row", "col")),
        check_vma=False,
    )
```
